256 devices in a mesh: dp: 2 (over y_hi), section: 16 (over y_lo, x, core), tensor: 8 (over z).
Axes of the slice: x: 4, y: 4 (y_hi: 2, y_lo: 2; y = y_hi * 2 + y_lo), z: 8, core: 2. Of those that a mesh axis runs over, the one named last changes fastest.
Arguments:
- hidden_in: float32 [32, 4, 16, 8192], P(('dp', 'section'), None, None, 'tensor'), parts along dimension 0
- norm_gain: float32 [32, 2, 8192], P(('dp', 'section'), None, 'tensor'), parts along dimension 0, may hold values from 0.1 to 1.9
- w_qkv: bfloat16 [32, 2, 8192, 1280], P(('dp', 'section'), None, 'tensor'), parts along dimension 0, may hold values from -0.109375 to 0.109375
- w_out: bfloat16 [32, 2, 1024, 8192], P(('dp', 'section'), None, None, 'tensor'), parts along dimension 0, may hold values from -0.1875 to 0.1875
- kv_cache: bfloat16 [32, 4, 4, 512, 256], P(('dp', 'section'), None, None, 'tensor'), parts along dimension 0
- parents: int32 [128, 16], P('dp'), parts along dimension 0, may hold values from 0 to 14, as said below
- lengths: int32 [128], P('dp'), parts along dimension 0, may hold values from 1 to 512, as said below
- assign: int32 [32, 4], P('dp'), parts along dimension 0, may hold values from 0 to 63, as said below
Outputs:
- hidden_out: float32 [32, 4, 16, 8192], P(('dp', 'section'), None, None, 'tensor'), parts along dimension 0
The draws below stay inside these ranges and needn't reach their ends.
There are 2 independent parts, one for each index of `dp`. The reference program is written for one: setup_inputs(seed, part) draws one part's arguments, and reference() takes and returns one part's arrays. A program takes and returns all parts, laid end to end along the dimension named above; each array names one. Nothing has to cross between parts.
Inputs may be any that keep to these rules, and one draw needn't show every extreme that they name: `parents`: node 0 is the root and its entry is 0; node a > 0 has a parent below a; the last node's parent is node 14. `lengths`: some request has length 512. `assign`: every request id appears exactly once.
All inputs are finite; a program needn't handle non-finite values.
Results may differ from the reference program's by a relative error of at most 0.0095.
Values may be sent and summed in bfloat16 or wider, within the bound.
No kernel may reach another device: no remote copies, remote signals or barrier semaphores. Data moves between devices by JAX's collectives and lax.ppermute only.
A program may use at most 64 MiB of HBM per device.

```python
import jax
import jax.numpy as jnp
from jax import lax

D = 8192
QH = 8
HS = 128
TREE = 16
LAYERS_SECTION = 2
STEPS = 4
R_MB = 4
CTX = 512
MB = 16
REQS = 64
QKV = 1280
HD = 1024


def draw_hidden_in(key, part):
    key = jax.random.fold_in(key, 15)
    shape = (MB, R_MB, TREE, D)
    feature = jnp.arange(D, dtype=jnp.float32) / (D - 1)
    base = jax.random.normal(jax.random.fold_in(key, 1), shape, jnp.float32)
    return base * jnp.exp(jnp.log(10.0) * feature)


def draw_kv_cache(key, part):
    key = jax.random.fold_in(key, 11)
    shape = (MB, STEPS, R_MB, CTX, 2 * HS)
    base = jax.random.normal(jax.random.fold_in(key, 1), shape, jnp.float32)
    key_side = base[..., :HS] * 1.7
    return jnp.concatenate([key_side, base[..., HS:]], axis=-1).astype(jnp.bfloat16)


def draw_parents(key, part):
    key = jax.random.fold_in(key, 12)
    node_index = jnp.arange(TREE, dtype=jnp.int32)[None, :]
    raw_bits = jax.random.randint(key, (REQS, TREE), 0, 1 << 20)
    chosen = raw_bits % jnp.maximum(node_index, 1)
    return jnp.where(node_index == TREE - 1, TREE - 2, chosen).astype(jnp.int32)


def draw_lengths(key, part):
    key = jax.random.fold_in(key, 13)
    raw_lengths = jax.random.randint(jax.random.fold_in(key, 1), (REQS,), 1, CTX + 1)
    longest = jax.random.randint(jax.random.fold_in(key, 2), (), 0, REQS)
    return jnp.where(jnp.arange(REQS, dtype=jnp.int32) == longest, CTX, raw_lengths).astype(jnp.int32)


def draw_assign(key, part):
    key = jax.random.fold_in(key, 14)
    return jax.random.permutation(key, REQS).astype(jnp.int32).reshape(MB, R_MB)


def levels(rng, extent, cuts, least, high):
    level = 1.0
    for axis_at, shards_of in cuts:
        steps = jax.random.uniform(jax.random.fold_in(jax.random.fold_in(rng, 6), axis_at), (shards_of,), jnp.float32, least / len(cuts), high / len(cuts))
        level = level * jnp.repeat(jnp.exp(steps), extent[axis_at] // shards_of).reshape((-1,) + (1,) * (len(extent) - 1 - axis_at))
    return level


def centred(own_key, dims, width, limit, cuts=(), kind=jnp.bfloat16):
    factor_of = levels(own_key, dims, cuts, -0.22, 0.18) if cuts else 1.0
    entries = jax.random.normal(own_key, dims, jnp.float32) * width * factor_of
    return jnp.minimum(jnp.maximum(entries, -limit), limit).astype(kind)


def setup_inputs(seed: int = 0, part: int = 0) -> dict:
    key_of = jax.random.split(jax.random.key(seed), 9)
    part_splits = jax.random.split(jax.random.fold_in(key_of[8], part), 9)
    return {
        "hidden_in": draw_hidden_in(jax.random.fold_in(jax.random.fold_in(key_of[8], part), 71), part),
        "norm_gain": jnp.clip(1.0 + 0.18 * jax.random.normal(part_splits[1], (MB, LAYERS_SECTION, D), jnp.float32), 0.1, 1.9),
        "w_qkv": centred(part_splits[2], (MB, LAYERS_SECTION, D, QKV), (D // 3) ** -0.5, 0.109375, ((0, 16), (2, 8))),
        "w_out": centred(part_splits[3], (MB, LAYERS_SECTION, HD, D), HD ** -0.5, 0.1875, ((0, 16), (3, 8))),
        "kv_cache": draw_kv_cache(jax.random.fold_in(jax.random.fold_in(key_of[8], part), 71), part),
        "parents": draw_parents(jax.random.fold_in(jax.random.fold_in(key_of[8], part), 71), part),
        "lengths": draw_lengths(jax.random.fold_in(jax.random.fold_in(key_of[8], part), 71), part),
        "assign": draw_assign(jax.random.fold_in(jax.random.fold_in(key_of[8], part), 71), part),
    }


epsilon = 1e-05
lowest = -1e+30

def rounded(values):
    return lax.optimization_barrier(values.astype(jnp.bfloat16)).astype(jnp.float32)

def ancestors(parent_rows):
    node_count = parent_rows.shape[1]
    identity = jnp.eye(node_count, dtype=jnp.float32)
    ancestor_rows = [jnp.broadcast_to(identity[0], (parent_rows.shape[0], node_count))]
    for node_index in range(1, node_count):
        onehot = (parent_rows[:, node_index][:, None] == jnp.arange(node_index, dtype=jnp.int32)[None, :]).astype(jnp.float32)
        earlier = jnp.stack(ancestor_rows, axis=1)
        ancestor_rows.append(jnp.einsum('rn,rnt->rt', onehot, earlier) + identity[node_index])
    return jnp.stack(ancestor_rows, axis=1) > 0.5

def layer(state, gain_row, weight_in, weight_out, cache_now, length_rows, visible):
    batch_rows, tree_size, width_all = state.shape
    factor = lax.rsqrt(lax.optimization_barrier(jnp.mean(state * state, axis=-1)) + epsilon)
    normed = (state * factor[..., None] * gain_row).astype(jnp.bfloat16)
    projected = rounded(jnp.dot(normed.reshape(-1, width_all), weight_in, preferred_element_type=jnp.float32))
    projected = projected.reshape(batch_rows, tree_size, QH + 2, HS)
    queries = projected[:, :, :QH]
    tree_keys = projected[:, :, QH]
    tree_values = projected[:, :, QH + 1]
    cache_keys = cache_now[..., :HS].astype(jnp.float32)
    cache_values = cache_now[..., HS:].astype(jnp.float32)
    scaling = HS ** (-0.5)
    cache_scores = jnp.einsum('rthe,rce->rthc', queries, cache_keys) * scaling
    tree_scores = jnp.einsum('rthe,rse->rths', queries, tree_keys) * scaling
    live_keys = jnp.arange(CTX, dtype=jnp.int32)[None, :] < length_rows[:, None]
    live_full = live_keys[:, None, None, :]
    tree_full = visible[:, :, None, :]
    cache_masked = jnp.where(live_full, cache_scores, lowest)
    tree_masked = jnp.where(tree_full, tree_scores, lowest)
    joint_max = jnp.maximum(lax.optimization_barrier(jnp.max(cache_masked, axis=-1)), lax.optimization_barrier(jnp.max(tree_masked, axis=-1)))
    cache_weights = jnp.exp(cache_masked - joint_max[..., None]) * live_full.astype(jnp.float32)
    tree_weights = jnp.exp(tree_masked - joint_max[..., None]) * tree_full.astype(jnp.float32)
    row_sum = lax.optimization_barrier(jnp.sum(cache_weights, axis=-1)) + lax.optimization_barrier(jnp.sum(tree_weights, axis=-1))
    weighted = jnp.einsum('rthc,rce->rthe', rounded(cache_weights), cache_values)
    weighted = weighted + jnp.einsum('rths,rse->rthe', rounded(tree_weights), tree_values)
    attended = (weighted / row_sum[..., None]).astype(jnp.bfloat16).reshape(batch_rows * tree_size, QH * HS)
    update = jnp.dot(attended, weight_out, preferred_element_type=jnp.float32)
    return state + update.reshape(state.shape)

def reference(hidden_in, norm_gain, w_qkv, w_out, kv_cache, parents, lengths, assign):
    section_list = jnp.arange(MB, dtype=jnp.int32)
    state = hidden_in
    for step_index in range(STEPS):

        def one_section(section_index, current=state, step_now=step_index):
            held_batch = (section_index - step_now) % MB
            which = (section_index < step_now).astype(jnp.int32)
            request_ids = assign[held_batch]
            visible = ancestors(parents[request_ids])
            return layer(current[section_index], norm_gain[section_index, which], w_qkv[section_index, which], w_out[section_index, which], kv_cache[section_index, step_now], lengths[request_ids], visible)
        state = lax.map(one_section, section_list)
        state = jnp.roll(state, 1, axis=0)
    return state
```

```python
import functools

import jax
import jax.numpy as jnp
from jax import lax
from jax.experimental import pallas as pl
from jax.experimental.pallas import tpu as pltpu
from jax.sharding import PartitionSpec as P

bf16 = jnp.bfloat16
f32 = jnp.float32

D = 8192
epsilon = 1e-05
lowest = -1e30
largest = 3.3e38

TREE = 16
HEAD = 128
BOTH = 2 * HEAD
HALF = 512
MIX = 768
PIECE = 896
CHUNKS = 8
VMEM_LIMIT = 16 * 1024 * 1024

VMEM = pl.BlockSpec(memory_space=pltpu.VMEM)
FAR = pl.BlockSpec(memory_space=pltpu.HBM)
PARAMS = pltpu.CompilerParams(vmem_limit_bytes=VMEM_LIMIT)


def layer_of(step):
    return (lax.axis_index("section") < step).astype(jnp.int32)


def loads(source, target, sems):
    count = sems.shape[0]
    rows = target.shape[0] // count
    return [
        pltpu.make_async_copy(
            source.at[pl.ds(part * rows, rows), :],
            target.at[pl.ds(part * rows, rows), :],
            sems.at[part],
        )
        for part in range(count)
    ]


def write_pieces(out_ref, raw, state):
    square = jnp.sum(state * state, axis=-1, keepdims=True)
    high = jnp.minimum(square, largest).astype(bf16)
    low = (square - high.astype(f32)).astype(bf16)
    lane = lax.broadcasted_iota(jnp.int32, (state.shape[0], HEAD), 1)
    pair = jnp.where(lane < HEAD // 2, high.astype(f32), low.astype(f32)).astype(bf16)
    raw = raw.astype(bf16)
    for slot in range(out_ref.shape[0] // 2):
        here = slice(slot * TREE, (slot + 1) * TREE)
        for half in range(2):
            out_ref[2 * slot + half, :, :HALF] = raw[here, half * HALF : (half + 1) * HALF]
            out_ref[2 * slot + half, :, HALF:MIX] = raw[here, 2 * HALF :]
            out_ref[2 * slot + half, :, MIX:PIECE] = pair[here]


def write_cache(out_ref, cache_ref, step):
    for slot in range(cache_ref.shape[1]):
        for chunk in range(cache_ref.shape[2] // TREE):
            block = cache_ref[step, slot, chunk * TREE : (chunk + 1) * TREE, :]
            start = PIECE + chunk * BOTH
            for half in range(2):
                out_ref[2 * slot + half, :, start : start + BOTH] = block


def first_kernel(
    assign_far, parents_far, lengths_far, state_far, gain_far, weight_far, cache_far,
    out_ref, state_ref, table_ref, gain_ref, weight_ref, cache_ref,
    assign_ref, parents_ref, lengths_ref, rows, sems, more,
):
    layers = weight_ref.shape[0]
    weight_copies = [
        loads(weight_far.at[0, layer], weight_ref.at[layer], sems.at[layer])
        for layer in range(layers)
    ]
    other = [
        pltpu.make_async_copy(source, target, more.at[index])
        for index, (source, target) in enumerate(
            (
                (assign_far, assign_ref),
                (parents_far, parents_ref),
                (lengths_far, lengths_ref),
                (state_far.at[0], state_ref),
                (gain_far.at[0], gain_ref),
                (cache_far.at[0], cache_ref),
            )
        )
    ]
    for copy in other[:5] + weight_copies[0] + other[5:] + sum(weight_copies[1:], []):
        copy.start()
    for copy in other[:3]:
        copy.wait()
    batches = assign_ref.shape[1]
    section = lax.axis_index("section")
    slot = lax.axis_index("tensor") // 2
    lane = lax.broadcasted_iota(jnp.int32, (1, HEAD), 1)
    steps = range(table_ref.shape[0])
    held = [lax.rem(section - step + batches, batches) for step in steps]
    request = [assign_ref[slot, held[step]] for step in steps]
    for step in steps:
        rows[step, pl.ds(0, 1), :] = jnp.where(lane == 0, 1.0, 0.0)
    for node in range(1, TREE):
        parents = [parents_ref[node, request[step]] for step in steps]
        above = [rows[step, pl.ds(parents[step], 1), :] for step in steps]
        for step in steps:
            rows[step, pl.ds(node, 1), :] = jnp.where(lane == node, 1.0, above[step])
    for step in steps:
        live = lengths_ref[request[step]].astype(f32)
        table_ref[step] = jnp.where(lane < TREE, rows[step], live)
    other[3].wait()
    other[4].wait()
    slots, tree, width = state_ref.shape
    state = state_ref[...].reshape(slots * tree, width)
    scaled = (state * gain_ref[0:1, :]).astype(bf16)
    depth = width // len(weight_copies[0])
    raw = jnp.zeros((slots * tree, weight_ref.shape[2]), f32)
    for part, copy in enumerate(weight_copies[0]):
        copy.wait()
        span = slice(part * depth, (part + 1) * depth)
        raw = raw + jnp.dot(scaled[:, span], weight_ref[0, span, :], preferred_element_type=f32)
    write_pieces(out_ref, raw, state)
    other[5].wait()
    write_cache(out_ref, cache_ref, 0)
    for copy in sum(weight_copies[1:], []):
        copy.wait()


def first(assign, parents, lengths, hidden, gain, weight, cache):
    _, slots, tree, width = hidden.shape
    steps, _, span = cache.shape[1:4]
    return pl.pallas_call(
        first_kernel,
        out_shape=(
            jax.ShapeDtypeStruct((2 * slots, TREE, PIECE + span // TREE * BOTH), bf16),
            pltpu.VMEM((slots, tree, width), f32),
            pltpu.VMEM((steps, TREE, HEAD), f32),
            pltpu.VMEM(gain.shape[1:], f32),
            pltpu.VMEM(weight.shape[1:], bf16),
            pltpu.VMEM(cache.shape[1:], bf16),
        ),
        in_specs=[FAR] * 7,
        out_specs=(VMEM,) * 6,
        scratch_shapes=[
            pltpu.SMEM(assign.shape[::-1], jnp.int32),
            pltpu.SMEM(parents.shape[::-1], jnp.int32),
            pltpu.SMEM(lengths.shape, jnp.int32),
            pltpu.VMEM((steps, TREE, HEAD), f32),
            pltpu.SemaphoreType.DMA((weight.shape[1], CHUNKS)),
            pltpu.SemaphoreType.DMA((6,)),
        ],
        compiler_params=PARAMS,
    )(*(far(value) for value in (assign.T, parents.T, lengths, hidden, gain, weight, cache)))


def project_kernel(state_ref, gain_ref, weight_ref, cache_ref, out_ref, *, step):
    slots, tree, width = state_ref.shape
    state = state_ref[...].reshape(slots * tree, width)
    which = layer_of(step)
    scaled = (state * gain_ref[pl.ds(which, 1), :]).astype(bf16)
    raw = jnp.dot(scaled, weight_ref[which], preferred_element_type=f32)
    write_pieces(out_ref, raw, state)
    write_cache(out_ref, cache_ref, step)


def project(state, gain, weight, cache, step):
    slots, span = cache.shape[1:3]
    return pl.pallas_call(
        functools.partial(project_kernel, step=step),
        out_shape=jax.ShapeDtypeStruct((2 * slots, TREE, PIECE + span // TREE * BOTH), bf16),
        in_specs=[VMEM] * 4,
        out_specs=VMEM,
        compiler_params=PARAMS,
    )(state, gain, weight, cache)


def attend_kernel(got_ref, table_ref, *refs, step):
    if step:
        (out_ref,) = refs
        copies = []
    else:
        weight_far, out_ref, weight_ref, sems = refs
        copies = sum(
            (
                loads(weight_far.at[0, layer], weight_ref.at[layer], sems.at[layer])
                for layer in range(weight_ref.shape[0])
            ),
            [],
        )
    for copy in copies:
        copy.start()
    total = jnp.sum(got_ref[:, :, :PIECE].astype(f32), axis=0)
    square = total[:, MIX : MIX + 1] + total[:, MIX + HEAD // 2 : MIX + HEAD // 2 + 1]
    factor = lax.rsqrt(square / D + epsilon)
    projected = (total[:, :MIX] * factor).astype(bf16)
    heads = HALF // HEAD
    queries = jnp.concatenate(
        [projected[:, h * HEAD : (h + 1) * HEAD] for h in range(heads)], axis=0
    )
    tree_keys = projected[:, HALF : HALF + HEAD]
    tree_values = projected[:, HALF + HEAD :]
    keys, values = (
        jnp.concatenate(
            [
                got_ref[piece, :, start + side : start + side + HEAD]
                for piece in range(got_ref.shape[0])
                for start in range(PIECE, got_ref.shape[2], BOTH)
            ],
            axis=0,
        )
        for side in (0, HEAD)
    )
    contract = (((1,), (1,)), ((), ()))
    scaling = HEAD ** (-0.5)
    scores = lax.dot_general(queries, keys, contract, preferred_element_type=f32)
    tree_scores = lax.dot_general(queries, tree_keys, contract, preferred_element_type=f32)
    position = lax.broadcasted_iota(jnp.int32, scores.shape, 1)
    table = table_ref[step]
    live = table[0:1, TREE : TREE + 1].astype(jnp.int32)
    visible = jnp.concatenate([table[:, :TREE]] * heads, axis=0) > 0.5
    scores = jnp.where(position < live, scores * scaling, lowest)
    tree_scores = jnp.where(visible, tree_scores * scaling, lowest)
    row_max = jnp.maximum(
        jnp.max(scores, axis=-1, keepdims=True), jnp.max(tree_scores, axis=-1, keepdims=True)
    )
    weights = jnp.exp(scores - row_max)
    tree_weights = jnp.exp(tree_scores - row_max)
    row_sum = jnp.sum(weights, axis=-1, keepdims=True) + jnp.sum(
        tree_weights, axis=-1, keepdims=True
    )
    weighted = jnp.dot(weights.astype(bf16), values, preferred_element_type=f32)
    weighted = weighted + jnp.dot(
        tree_weights.astype(bf16), tree_values, preferred_element_type=f32
    )
    attended = (weighted / row_sum).astype(bf16)
    for h in range(heads):
        part = attended[h * TREE : (h + 1) * TREE]
        for piece in range(out_ref.shape[0]):
            out_ref[piece, :, h * HEAD : (h + 1) * HEAD] = part
    for copy in copies:
        copy.wait()


def attend(got, table, step, weight=None):
    out_shape = (jax.ShapeDtypeStruct((got.shape[0], TREE, HALF), bf16),)
    extra, scratch = (), []
    if weight is not None:
        out_shape += (pltpu.VMEM(weight.shape[1:], bf16),)
        extra = (far(weight),)
        scratch = [pltpu.SemaphoreType.DMA((weight.shape[1], CHUNKS))]
    return pl.pallas_call(
        functools.partial(attend_kernel, step=step),
        out_shape=out_shape,
        in_specs=[VMEM] * 2 + [FAR] * len(extra),
        out_specs=(VMEM,) * len(out_shape),
        scratch_shapes=scratch,
        compiler_params=PARAMS,
    )(got, table, *extra)


def update_kernel(state_ref, got_ref, weight_ref, out_ref, *, step):
    slots = got_ref.shape[0] // 2
    attended = jnp.concatenate(
        [jnp.concatenate([got_ref[2 * s], got_ref[2 * s + 1]], axis=1) for s in range(slots)],
        axis=0,
    )
    delta = jnp.dot(attended, weight_ref[layer_of(step)], preferred_element_type=f32)
    out_ref[...] = state_ref[...] + delta.reshape(out_ref.shape)


def update(state, got, weight, step):
    return pl.pallas_call(
        functools.partial(update_kernel, step=step),
        out_shape=jax.ShapeDtypeStruct(state.shape, f32),
        in_specs=[VMEM] * 3,
        out_specs=VMEM,
        compiler_params=PARAMS,
    )(state, got, weight)


def exchange(value):
    return lax.all_to_all(value, "tensor", 0, 0, tiled=True)


def far(value):
    return pltpu.with_memory_space_constraint(value, pltpu.HBM)


def body(hidden_in, norm_gain, w_qkv, w_out, kv_cache, parents, lengths, assign):
    sections = lax.axis_size("section")
    ring = [(s, (s + 1) % sections) for s in range(sections)]
    pieces, state, table, gain, weight_in, cache = first(
        assign, parents, lengths, hidden_in, norm_gain, w_qkv, kv_cache
    )
    weight_out = None
    for step in range(kv_cache.shape[1]):
        if step:
            pieces = project(state, gain, weight_in, cache, step)
        got = exchange(pieces)
        if step:
            (spread,) = attend(got, table, step)
        else:
            spread, weight_out = attend(got, table, step, w_out)
        state = update(state, exchange(spread), weight_out, step)
        state = lax.ppermute(state, "section", ring)
    return state[None]


def solution(mesh):
    in_specs = (
        P(("dp", "section"), None, None, "tensor"),
        P(("dp", "section"), None, "tensor"),
        P(("dp", "section"), None, "tensor", None),
        P(("dp", "section"), None, None, "tensor"),
        P(("dp", "section"), None, None, "tensor", None),
        P("dp", None),
        P("dp"),
        P("dp", None),
    )
    out_specs = P(("dp", "section"), None, None, "tensor")
    return jax.shard_map(body, mesh=mesh, in_specs=in_specs, out_specs=out_specs, check_vma=False)
```

```python
import functools

import jax
import jax.numpy as jnp
from jax import lax
from jax.experimental import pallas as pl
from jax.experimental.pallas import tpu as pltpu
from jax.sharding import PartitionSpec as P

bf16 = jnp.bfloat16
f32 = jnp.float32

D = 8192
epsilon = 1e-05
lowest = -1e30
largest = 3.3e38

TREE = 16
HEAD = 128
BOTH = 2 * HEAD
HALF = 512
MIX = 768
PIECE = 896
CHUNKS = 8
TOP = 125.0
VMEM_LIMIT = 16 * 1024 * 1024

VMEM = pl.BlockSpec(memory_space=pltpu.VMEM)
FAR = pl.BlockSpec(memory_space=pltpu.HBM)
PARAMS = pltpu.CompilerParams(vmem_limit_bytes=VMEM_LIMIT)


def layer_of(step):
    return (lax.axis_index("section") < step).astype(jnp.int32)


def loads(source, target, sems):
    count = sems.shape[0]
    rows = target.shape[0] // count
    return [
        pltpu.make_async_copy(
            source.at[pl.ds(part * rows, rows), :],
            target.at[pl.ds(part * rows, rows), :],
            sems.at[part],
        )
        for part in range(count)
    ]


def write_pieces(out_ref, raw, state):
    square = jnp.sum(state * state, axis=-1, keepdims=True)
    high = jnp.minimum(square, largest).astype(bf16)
    low = (square - high.astype(f32)).astype(bf16)
    lane = lax.broadcasted_iota(jnp.int32, (state.shape[0], HEAD), 1)
    pair = jnp.where(lane < HEAD // 2, high.astype(f32), low.astype(f32)).astype(bf16)
    raw = raw.astype(bf16)
    for slot in range(out_ref.shape[0] // 2):
        here = slice(slot * TREE, (slot + 1) * TREE)
        for half in range(2):
            out_ref[2 * slot + half, :, :HALF] = raw[here, half * HALF : (half + 1) * HALF]
            out_ref[2 * slot + half, :, HALF:MIX] = raw[here, 2 * HALF :]
            out_ref[2 * slot + half, :, MIX:PIECE] = pair[here]


def chunks_of(cache_ref):
    return range(cache_ref.shape[2] // TREE)


def write_cache(out_ref, cache_ref, step, start):
    for slot in range(cache_ref.shape[1]):
        for chunk in chunks_of(cache_ref):
            block = cache_ref[step, slot, chunk * TREE : (chunk + 1) * TREE, :]
            place = start + chunk * BOTH
            for half in range(2):
                out_ref[2 * slot + half, :, place : place + BOTH] = block


def write_sides(out_ref, cache_ref, step, start):
    for slot in range(cache_ref.shape[1]):
        for chunk in chunks_of(cache_ref):
            here = slice(chunk * TREE, (chunk + 1) * TREE)
            place = start + chunk * HEAD
            for half in range(2):
                out_ref[2 * slot + half, :, place : place + HEAD] = cache_ref[
                    step, slot, here, half * HEAD : (half + 1) * HEAD
                ]


def first_kernel(
    assign_far, parents_far, lengths_far, state_far, gain_far, weight_far, cache_far,
    out_ref, state_ref, table_ref, gain_ref, weight_ref, cache_ref,
    assign_ref, parents_ref, lengths_ref, rows, sems, more,
):
    weight_copies = loads(weight_far.at[0, 0], weight_ref, sems)
    other = [
        pltpu.make_async_copy(source, target, more.at[index])
        for index, (source, target) in enumerate(
            (
                (assign_far, assign_ref),
                (parents_far, parents_ref),
                (lengths_far, lengths_ref),
                (state_far, state_ref),
                (gain_far.at[0], gain_ref),
                (cache_far.at[0], cache_ref),
            )
        )
    ]
    for copy in other[:5] + weight_copies + other[5:]:
        copy.start()
    for copy in other[:3]:
        copy.wait()
    batches = assign_ref.shape[1]
    section = lax.axis_index("section")
    slot = lax.axis_index("tensor") // 2
    lane = lax.broadcasted_iota(jnp.int32, (1, HEAD), 1)
    steps = range(table_ref.shape[0])
    held = [lax.rem(section - step + batches, batches) for step in steps]
    request = [assign_ref[slot, held[step]] for step in steps]
    for step in steps:
        rows[step, pl.ds(0, 1), :] = jnp.where(lane == 0, 1.0, 0.0)
    for node in range(1, TREE):
        parents = [parents_ref[node, request[step]] for step in steps]
        above = [rows[step, pl.ds(parents[step], 1), :] for step in steps]
        for step in steps:
            rows[step, pl.ds(node, 1), :] = jnp.where(lane == node, 1.0, above[step])
    for step in steps:
        live = lengths_ref[request[step]].astype(f32)
        table_ref[step] = jnp.where(lane < TREE, rows[step], live)
    other[3].wait()
    other[4].wait()
    width = state_ref.shape[1]
    state = state_ref[...]
    scaled = (state * gain_ref[0:1, :]).astype(bf16)
    depth = width // len(weight_copies)
    raw = jnp.zeros((state.shape[0], weight_ref.shape[1]), f32)
    for part, copy in enumerate(weight_copies):
        copy.wait()
        span = slice(part * depth, (part + 1) * depth)
        raw = raw + jnp.dot(scaled[:, span], weight_ref[span, :], preferred_element_type=f32)
    write_pieces(out_ref, raw, state)
    other[5].wait()
    write_cache(out_ref, cache_ref, 0, PIECE)


def first(assign, parents, lengths, hidden, gain, weight, cache):
    _, slots, tree, width = hidden.shape
    steps, _, span = cache.shape[1:4]
    rows = hidden.reshape(slots * tree, width)
    return pl.pallas_call(
        first_kernel,
        out_shape=(
            jax.ShapeDtypeStruct((2 * slots, TREE, PIECE + span // TREE * BOTH), bf16),
            pltpu.VMEM((slots * tree, width), f32),
            pltpu.VMEM((steps, TREE, HEAD), f32),
            pltpu.VMEM(gain.shape[1:], f32),
            pltpu.VMEM(weight.shape[2:], bf16),
            pltpu.VMEM(cache.shape[1:], bf16),
        ),
        in_specs=[FAR] * 7,
        out_specs=(VMEM,) * 6,
        scratch_shapes=[
            pltpu.SMEM(assign.shape[::-1], jnp.int32),
            pltpu.SMEM(parents.shape[::-1], jnp.int32),
            pltpu.SMEM(lengths.shape, jnp.int32),
            pltpu.VMEM((steps, TREE, HEAD), f32),
            pltpu.SemaphoreType.DMA((CHUNKS,)),
            pltpu.SemaphoreType.DMA((6,)),
        ],
        compiler_params=PARAMS,
    )(*map(far, (assign.T, parents.T, lengths, rows, gain, weight, cache)))


def rest_kernel(in_far, out_far, _, in_ref, out_ref, sems):
    copies = loads(in_far.at[0, 1], in_ref, sems.at[0]) + loads(out_far.at[0, 1], out_ref, sems.at[1])
    for copy in copies:
        copy.start()
    for copy in copies:
        copy.wait()


def rest(weight_in, weight_out, after):
    return pl.pallas_call(
        rest_kernel,
        out_shape=tuple(pltpu.VMEM(w.shape[2:], bf16) for w in (weight_in, weight_out)),
        in_specs=[FAR] * 2 + [VMEM],
        out_specs=(VMEM,) * 2,
        scratch_shapes=[pltpu.SemaphoreType.DMA((2, CHUNKS))],
        compiler_params=PARAMS,
    )(far(weight_in), far(weight_out), after)


def pick(step, act, layers):
    if len(layers) == 1:
        return act(layers[0])
    which = layer_of(step)
    for index, layer in enumerate(layers):
        pl.when(which == index)(functools.partial(act, layer))


def unit_of(power):
    return jnp.exp2(power) / jnp.where(power < TOP, 32767.0, 4095.0)


def pack(packed_ref, state):
    width = state.shape[1]
    peak = jnp.max(jnp.abs(state), axis=-1, keepdims=True)
    power = jnp.clip(jnp.ceil(jnp.log2(jnp.maximum(peak, 1e-37))), -TOP, TOP)
    ratio = state * jnp.exp2(-power) * jnp.where(power < TOP, 32767.0, 4095.0)
    steps = jnp.clip(jnp.round(ratio), -32767.0, 32767.0)
    packed_ref[:, :width] = steps.astype(jnp.int32).astype(jnp.int16)
    powers = jnp.broadcast_to(power.astype(jnp.int32), (state.shape[0], HEAD))
    packed_ref[:, width:] = powers.astype(jnp.int16)


def unpack(packed_ref):
    width = packed_ref.shape[1] - HEAD
    power = packed_ref[:, width:].astype(jnp.int32).astype(f32)[:, :1]
    return packed_ref[:, :width].astype(jnp.int32).astype(f32) * unit_of(power)


def expand_kernel(packed_ref, out_ref):
    out_ref[...] = unpack(packed_ref)


def expand(packed):
    rows, width = packed.shape
    return pl.pallas_call(
        expand_kernel,
        out_shape=jax.ShapeDtypeStruct((rows, width - HEAD), f32),
        in_specs=[VMEM],
        out_specs=VMEM,
        compiler_params=PARAMS,
    )(packed)


def project_kernel(packed_ref, mine_ref, come_ref, gain_ref, *refs, step):
    *weight_refs, out_ref, state_ref, sides_ref = refs
    side = lax.rem(lax.axis_index("tensor"), 2)
    sides_ref[side] = mine_ref[...]
    sides_ref[1 - side] = come_ref[...]
    state = unpack(packed_ref)
    state_ref[...] = state
    scaled = (state * gain_ref[pl.ds(layer_of(step), 1), :]).astype(bf16)

    def act(weight_ref):
        raw = jnp.dot(scaled, weight_ref[...], preferred_element_type=f32)
        write_pieces(out_ref, raw, state)

    pick(step, act, weight_refs)


def project(packed, mine, come, gain, weights, step):
    rows, width = packed.shape
    return pl.pallas_call(
        functools.partial(project_kernel, step=step),
        out_shape=(
            jax.ShapeDtypeStruct((mine.shape[0], TREE, PIECE), bf16),
            jax.ShapeDtypeStruct((rows, width - HEAD), f32),
            jax.ShapeDtypeStruct((2,) + mine.shape, bf16),
        ),
        in_specs=[VMEM] * (4 + len(weights)),
        out_specs=(VMEM,) * 3,
        compiler_params=PARAMS,
    )(packed, mine, come, gain, *weights)


def attend_kernel(got_ref, table_ref, cache_ref, *refs, step):
    if step:
        sides_ref, out_ref = refs
        copies = []
    else:
        weight_far, out_ref, weight_ref, sems = refs
        copies = loads(weight_far.at[0, 0], weight_ref, sems)
    for copy in copies:
        copy.start()
    total = jnp.sum(got_ref[:, :, :PIECE].astype(f32), axis=0)
    square = total[:, MIX : MIX + 1] + total[:, MIX + HEAD // 2 : MIX + HEAD // 2 + 1]
    factor = lax.rsqrt(square / D + epsilon)
    projected = (total[:, :MIX] * factor).astype(bf16)
    heads = HALF // HEAD
    queries = jnp.concatenate(
        [projected[:, h * HEAD : (h + 1) * HEAD] for h in range(heads)], axis=0
    )
    tree_keys = projected[:, HALF : HALF + HEAD]
    tree_values = projected[:, HALF + HEAD :]
    if step:
        blocks = [
            [
                sides_ref[side, piece, :, start : start + HEAD]
                for piece in range(sides_ref.shape[1])
                for start in range(0, sides_ref.shape[3], HEAD)
            ]
            for side in range(2)
        ]
    else:
        blocks = [
            [
                got_ref[piece, :, start + side * HEAD : start + (side + 1) * HEAD]
                for piece in range(got_ref.shape[0])
                for start in range(PIECE, got_ref.shape[2], BOTH)
            ]
            for side in range(2)
        ]
    keys, values = (jnp.concatenate(block, axis=0) for block in blocks)
    contract = (((1,), (1,)), ((), ()))
    scaling = HEAD ** (-0.5)
    scores = lax.dot_general(queries, keys, contract, preferred_element_type=f32)
    tree_scores = lax.dot_general(queries, tree_keys, contract, preferred_element_type=f32)
    position = lax.broadcasted_iota(jnp.int32, scores.shape, 1)
    table = table_ref[step]
    live = table[0:1, TREE : TREE + 1].astype(jnp.int32)
    visible = jnp.concatenate([table[:, :TREE]] * heads, axis=0) > 0.5
    scores = jnp.where(position < live, scores * scaling, lowest)
    tree_scores = jnp.where(visible, tree_scores * scaling, lowest)
    row_max = jnp.maximum(
        jnp.max(scores, axis=-1, keepdims=True), jnp.max(tree_scores, axis=-1, keepdims=True)
    )
    weights = jnp.exp(scores - row_max)
    tree_weights = jnp.exp(tree_scores - row_max)
    row_sum = jnp.sum(weights, axis=-1, keepdims=True) + jnp.sum(
        tree_weights, axis=-1, keepdims=True
    )
    weighted = jnp.dot(weights.astype(bf16), values, preferred_element_type=f32)
    weighted = weighted + jnp.dot(
        tree_weights.astype(bf16), tree_values, preferred_element_type=f32
    )
    attended = (weighted / row_sum).astype(bf16)
    for h in range(heads):
        part = attended[h * TREE : (h + 1) * TREE]
        for piece in range(out_ref.shape[0]):
            out_ref[piece, :, h * HEAD : (h + 1) * HEAD] = part
    if step + 1 < cache_ref.shape[0]:
        write_sides(out_ref, cache_ref, step + 1, HALF)
    for copy in copies:
        copy.wait()


def attend(got, table, cache, step, sides=None, weight=None):
    steps, _, span = cache.shape[:3]
    width = HALF + (span // TREE * HEAD if step + 1 < steps else 0)
    out_shape = (jax.ShapeDtypeStruct((got.shape[0], TREE, width), bf16),)
    extra, scratch = (sides,), []
    specs = [VMEM] * 4
    if weight is not None:
        out_shape += (pltpu.VMEM(weight.shape[2:], bf16),)
        extra = (far(weight),)
        specs[3] = FAR
        scratch = [pltpu.SemaphoreType.DMA((CHUNKS,))]
    return pl.pallas_call(
        functools.partial(attend_kernel, step=step),
        out_shape=out_shape,
        in_specs=specs,
        out_specs=(VMEM,) * len(out_shape),
        scratch_shapes=scratch,
        compiler_params=PARAMS,
    )(got, table, cache, *extra)


def update_kernel(state_ref, got_ref, *refs, step, last):
    if last:
        *weight_refs, out_ref = refs
    else:
        *weight_refs, out_ref, side_ref = refs
        side_ref[...] = got_ref[:, :, HALF:]
    attended = jnp.concatenate(
        [
            jnp.concatenate([got_ref[at, :, :HALF], got_ref[at + 1, :, :HALF]], axis=1)
            for at in range(0, got_ref.shape[0], 2)
        ],
        axis=0,
    )

    def act(weight_ref):
        delta = jnp.dot(attended, weight_ref[...], preferred_element_type=f32)
        pack(out_ref, state_ref[...] + delta)

    pick(step, act, weight_refs)


def update(state, got, weights, step):
    rows, width = state.shape
    count, tree, total = got.shape
    out_shape = (jax.ShapeDtypeStruct((rows, width + HEAD), jnp.int16),)
    last = total == HALF
    if not last:
        out_shape += (jax.ShapeDtypeStruct((count, tree, total - HALF), bf16),)
    return pl.pallas_call(
        functools.partial(update_kernel, step=step, last=last),
        out_shape=out_shape,
        in_specs=[VMEM] * (2 + len(weights)),
        out_specs=(VMEM,) * len(out_shape),
        compiler_params=PARAMS,
    )(state, got, *weights)


def exchange(value):
    return lax.all_to_all(value, "tensor", 0, 0, tiled=True)


def far(value):
    return pltpu.with_memory_space_constraint(value, pltpu.HBM)


def body(hidden_in, norm_gain, w_qkv, w_out, kv_cache, parents, lengths, assign):
    sections = lax.axis_size("section")
    ring = [(s, (s + 1) % sections) for s in range(sections)]
    pieces, state, table, gain, weight_in, cache = first(
        assign, parents, lengths, hidden_in, norm_gain, w_qkv, kv_cache
    )
    weights_in = (weight_in,)
    mates = [(t, t ^ 1) for t in range(pieces.shape[0])]
    for step in range(kv_cache.shape[1]):
        if step:
            pieces, state, sides = project(packed, mine, come, gain, weights_in, step)
            (spread,) = attend(exchange(pieces), table, cache, step, sides)
        else:
            spread, weight_out = attend(exchange(pieces), table, cache, step, weight=w_out)
            weights_out = (weight_out,)
        packed, *mine = update(state, exchange(spread), weights_out, step)
        if not step:
            more_in, more_out = rest(w_qkv, w_out, packed)
            weights_in += (more_in,)
            weights_out += (more_out,)
        packed = lax.ppermute(packed, "section", ring)
        if mine:
            (mine,) = mine
            come = lax.ppermute(mine, "tensor", mates)
    return expand(packed).reshape(hidden_in.shape)


def solution(mesh):
    in_specs = (
        P(("dp", "section"), None, None, "tensor"),
        P(("dp", "section"), None, "tensor"),
        P(("dp", "section"), None, "tensor", None),
        P(("dp", "section"), None, None, "tensor"),
        P(("dp", "section"), None, None, "tensor", None),
        P("dp", None),
        P("dp"),
        P("dp", None),
    )
    out_specs = P(("dp", "section"), None, None, "tensor")
    return jax.shard_map(body, mesh=mesh, in_specs=in_specs, out_specs=out_specs, check_vma=False)
```

```python
import functools

import jax
import jax.numpy as jnp
from jax import lax
from jax.experimental import pallas as pl
from jax.experimental.pallas import tpu as pltpu
from jax.sharding import PartitionSpec as P

bf16 = jnp.bfloat16
f32 = jnp.float32

D = 8192
epsilon = 1e-05
lowest = -1e30
largest = 3.3e38

TREE = 16
HEAD = 128
BOTH = 2 * HEAD
HALF = 512
MIX = 768
PIECE = 896
CHUNKS = 8
VMEM_LIMIT = 16 * 1024 * 1024

VMEM = pl.BlockSpec(memory_space=pltpu.VMEM)
FAR = pl.BlockSpec(memory_space=pltpu.HBM)
PARAMS = pltpu.CompilerParams(vmem_limit_bytes=VMEM_LIMIT)


def layer_of(step):
    return (lax.axis_index("section") < step).astype(jnp.int32)


def loads(source, target, sems):
    count = sems.shape[0]
    rows = target.shape[0] // count
    return [
        pltpu.make_async_copy(
            source.at[pl.ds(part * rows, rows), :],
            target.at[pl.ds(part * rows, rows), :],
            sems.at[part],
        )
        for part in range(count)
    ]


def write_pieces(out_ref, raw, state):
    square = jnp.sum(state * state, axis=-1, keepdims=True)
    high = jnp.minimum(square, largest).astype(bf16)
    low = (square - high.astype(f32)).astype(bf16)
    lane = lax.broadcasted_iota(jnp.int32, (state.shape[0], HEAD), 1)
    pair = jnp.where(lane < HEAD // 2, high.astype(f32), low.astype(f32)).astype(bf16)
    raw = raw.astype(bf16)
    for slot in range(out_ref.shape[0] // 2):
        here = slice(slot * TREE, (slot + 1) * TREE)
        for half in range(2):
            out_ref[2 * slot + half, :, :HALF] = raw[here, half * HALF : (half + 1) * HALF]
            out_ref[2 * slot + half, :, HALF:MIX] = raw[here, 2 * HALF :]
            out_ref[2 * slot + half, :, MIX:PIECE] = pair[here]


def chunks_of(cache_ref):
    return range(cache_ref.shape[2] // TREE)


def write_cache(out_ref, cache_ref, step, start):
    for slot in range(cache_ref.shape[1]):
        for chunk in chunks_of(cache_ref):
            block = cache_ref[step, slot, chunk * TREE : (chunk + 1) * TREE, :]
            place = start + chunk * BOTH
            for half in range(2):
                out_ref[2 * slot + half, :, place : place + BOTH] = block


def write_sides(out_ref, cache_ref, step, start):
    for slot in range(cache_ref.shape[1]):
        for chunk in chunks_of(cache_ref):
            here = slice(chunk * TREE, (chunk + 1) * TREE)
            place = start + chunk * HEAD
            for half in range(2):
                out_ref[2 * slot + half, :, place : place + HEAD] = cache_ref[
                    step, slot, here, half * HEAD : (half + 1) * HEAD
                ]


def first_kernel(
    assign_far, parents_far, lengths_far, state_far, gain_far, weight_far, cache_far,
    out_ref, state_ref, table_ref, gain_ref, weight_ref, cache_ref,
    assign_ref, parents_ref, lengths_ref, rows, sems, more,
):
    weight_copies = loads(weight_far.at[0, 0], weight_ref, sems)
    other = [
        pltpu.make_async_copy(source, target, more.at[index])
        for index, (source, target) in enumerate(
            (
                (assign_far, assign_ref),
                (parents_far, parents_ref),
                (lengths_far, lengths_ref),
                (state_far, state_ref),
                (gain_far.at[0], gain_ref),
                (cache_far.at[0], cache_ref),
            )
        )
    ]
    for copy in other[:5] + weight_copies + other[5:]:
        copy.start()
    for copy in other[:3]:
        copy.wait()
    batches = assign_ref.shape[1]
    section = lax.axis_index("section")
    slot = lax.axis_index("tensor") // 2
    lane = lax.broadcasted_iota(jnp.int32, (1, HEAD), 1)
    steps = range(table_ref.shape[0])
    held = [lax.rem(section - step + batches, batches) for step in steps]
    request = [assign_ref[slot, held[step]] for step in steps]
    for step in steps:
        rows[step, pl.ds(0, 1), :] = jnp.where(lane == 0, 1.0, 0.0)
    for node in range(1, TREE):
        parents = [parents_ref[node, request[step]] for step in steps]
        above = [rows[step, pl.ds(parents[step], 1), :] for step in steps]
        for step in steps:
            rows[step, pl.ds(node, 1), :] = jnp.where(lane == node, 1.0, above[step])
    for step in steps:
        live = lengths_ref[request[step]].astype(f32)
        table_ref[step] = jnp.where(lane < TREE, rows[step], live)
    other[3].wait()
    other[4].wait()
    width = state_ref.shape[1]
    state = state_ref[...]
    scaled = (state * gain_ref[0:1, :]).astype(bf16)
    depth = width // len(weight_copies)
    raw = jnp.zeros((state.shape[0], weight_ref.shape[1]), f32)
    for part, copy in enumerate(weight_copies):
        copy.wait()
        span = slice(part * depth, (part + 1) * depth)
        raw = raw + jnp.dot(scaled[:, span], weight_ref[span, :], preferred_element_type=f32)
    write_pieces(out_ref, raw, state)
    other[5].wait()
    write_cache(out_ref, cache_ref, 0, PIECE)


def first(assign, parents, lengths, hidden, gain, weight, cache):
    _, slots, tree, width = hidden.shape
    steps, _, span = cache.shape[1:4]
    rows = hidden.reshape(slots * tree, width)
    return pl.pallas_call(
        first_kernel,
        out_shape=(
            jax.ShapeDtypeStruct((2 * slots, TREE, PIECE + span // TREE * BOTH), bf16),
            pltpu.VMEM((slots * tree, width), f32),
            pltpu.VMEM((steps, TREE, HEAD), f32),
            pltpu.VMEM(gain.shape[1:], f32),
            pltpu.VMEM(weight.shape[2:], bf16),
            pltpu.VMEM(cache.shape[1:], bf16),
        ),
        in_specs=[FAR] * 7,
        out_specs=(VMEM,) * 6,
        scratch_shapes=[
            pltpu.SMEM(assign.shape[::-1], jnp.int32),
            pltpu.SMEM(parents.shape[::-1], jnp.int32),
            pltpu.SMEM(lengths.shape, jnp.int32),
            pltpu.VMEM((steps, TREE, HEAD), f32),
            pltpu.SemaphoreType.DMA((CHUNKS,)),
            pltpu.SemaphoreType.DMA((6,)),
        ],
        compiler_params=PARAMS,
    )(*map(far, (assign.T, parents.T, lengths, rows, gain, weight, cache)))


def rest_kernel(in_far, _, in_ref, sems):
    copies = loads(in_far.at[0, 1], in_ref, sems)
    for copy in copies:
        copy.start()
    for copy in copies:
        copy.wait()


def rest(weight_in, after):
    return pl.pallas_call(
        rest_kernel,
        out_shape=pltpu.VMEM(weight_in.shape[2:], bf16),
        in_specs=[FAR, VMEM],
        out_specs=VMEM,
        scratch_shapes=[pltpu.SemaphoreType.DMA((CHUNKS,))],
        compiler_params=PARAMS,
    )(far(weight_in), after)


def pick(step, act, layers):
    if len(layers) == 1:
        return act(layers[0])
    which = layer_of(step)
    for index, layer in enumerate(layers):
        pl.when(which == index)(functools.partial(act, layer))


def project_kernel(state_ref, mine_ref, come_ref, gain_ref, *refs, step):
    *weight_refs, out_ref, sides_ref = refs
    side = lax.rem(lax.axis_index("tensor"), 2)
    sides_ref[side] = mine_ref[...]
    sides_ref[1 - side] = come_ref[...]
    state = state_ref[...]
    scaled = (state * gain_ref[pl.ds(layer_of(step), 1), :]).astype(bf16)

    def act(weight_ref):
        raw = jnp.dot(scaled, weight_ref[...], preferred_element_type=f32)
        write_pieces(out_ref, raw, state)

    pick(step, act, weight_refs)


def project(state, mine, come, gain, weights, step):
    return pl.pallas_call(
        functools.partial(project_kernel, step=step),
        out_shape=(
            jax.ShapeDtypeStruct((mine.shape[0], TREE, PIECE), bf16),
            jax.ShapeDtypeStruct((2,) + mine.shape, bf16),
        ),
        in_specs=[VMEM] * (4 + len(weights)),
        out_specs=(VMEM,) * 2,
        compiler_params=PARAMS,
    )(state, mine, come, gain, *weights)


def attend_kernel(got_ref, table_ref, cache_ref, *refs, step):
    *sides_ref, out_ref = refs
    total = jnp.sum(got_ref[:, :, :PIECE].astype(f32), axis=0)
    square = total[:, MIX : MIX + 1] + total[:, MIX + HEAD // 2 : MIX + HEAD // 2 + 1]
    factor = lax.rsqrt(square / D + epsilon)
    projected = (total[:, :MIX] * factor).astype(bf16)
    heads = HALF // HEAD
    queries = jnp.concatenate(
        [projected[:, h * HEAD : (h + 1) * HEAD] for h in range(heads)], axis=0
    )
    tree_keys = projected[:, HALF : HALF + HEAD]
    tree_values = projected[:, HALF + HEAD :]
    if step:
        blocks = [
            [
                sides_ref[0][side, piece, :, start : start + HEAD]
                for piece in range(sides_ref[0].shape[1])
                for start in range(0, sides_ref[0].shape[3], HEAD)
            ]
            for side in range(2)
        ]
    else:
        blocks = [
            [
                got_ref[piece, :, start + side * HEAD : start + (side + 1) * HEAD]
                for piece in range(got_ref.shape[0])
                for start in range(PIECE, got_ref.shape[2], BOTH)
            ]
            for side in range(2)
        ]
    keys, values = (jnp.concatenate(block, axis=0) for block in blocks)
    contract = (((1,), (1,)), ((), ()))
    scaling = HEAD ** (-0.5)
    scores = lax.dot_general(queries, keys, contract, preferred_element_type=f32)
    tree_scores = lax.dot_general(queries, tree_keys, contract, preferred_element_type=f32)
    position = lax.broadcasted_iota(jnp.int32, scores.shape, 1)
    table = table_ref[step]
    live = table[0:1, TREE : TREE + 1].astype(jnp.int32)
    visible = jnp.concatenate([table[:, :TREE]] * heads, axis=0) > 0.5
    scores = jnp.where(position < live, scores * scaling, lowest)
    tree_scores = jnp.where(visible, tree_scores * scaling, lowest)
    row_max = jnp.maximum(
        jnp.max(scores, axis=-1, keepdims=True), jnp.max(tree_scores, axis=-1, keepdims=True)
    )
    weights = jnp.exp(scores - row_max)
    tree_weights = jnp.exp(tree_scores - row_max)
    row_sum = jnp.sum(weights, axis=-1, keepdims=True) + jnp.sum(
        tree_weights, axis=-1, keepdims=True
    )
    weighted = jnp.dot(weights.astype(bf16), values, preferred_element_type=f32)
    weighted = weighted + jnp.dot(
        tree_weights.astype(bf16), tree_values, preferred_element_type=f32
    )
    attended = (weighted / row_sum).astype(bf16)
    for h in range(heads):
        part = attended[h * TREE : (h + 1) * TREE]
        for piece in range(out_ref.shape[0]):
            out_ref[piece, :, h * HEAD : (h + 1) * HEAD] = part
    if step + 1 < cache_ref.shape[0]:
        write_sides(out_ref, cache_ref, step + 1, HALF)


def attend(got, table, cache, step, sides=()):
    steps, _, span = cache.shape[:3]
    width = HALF + (span // TREE * HEAD if step + 1 < steps else 0)
    return pl.pallas_call(
        functools.partial(attend_kernel, step=step),
        out_shape=jax.ShapeDtypeStruct((got.shape[0], TREE, width), bf16),
        in_specs=[VMEM] * (3 + len(sides)),
        out_specs=VMEM,
        compiler_params=PARAMS,
    )(got, table, cache, *sides)


def update_kernel(state_ref, got_ref, weight_ref, *refs, step, last):
    if last:
        (out_ref,) = refs
    else:
        out_ref, side_ref = refs
        side_ref[...] = got_ref[:, :, HALF:]
    attended = jnp.concatenate(
        [
            jnp.concatenate([got_ref[at, :, :HALF], got_ref[at + 1, :, :HALF]], axis=1)
            for at in range(0, got_ref.shape[0], 2)
        ],
        axis=0,
    )

    delta = jnp.dot(attended, weight_ref[0, layer_of(step)], preferred_element_type=f32)
    out_ref[...] = state_ref[...] + delta


def update(state, got, weight, step):
    count, tree, total = got.shape
    out_shape = (jax.ShapeDtypeStruct(state.shape, f32),)
    last = total == HALF
    if not last:
        out_shape += (jax.ShapeDtypeStruct((count, tree, total - HALF), bf16),)
    return pl.pallas_call(
        functools.partial(update_kernel, step=step, last=last),
        out_shape=out_shape,
        in_specs=[VMEM] * 3,
        out_specs=(VMEM,) * len(out_shape),
        compiler_params=PARAMS,
    )(state, got, weight)


def exchange(value):
    return lax.all_to_all(value, "tensor", 0, 0, tiled=True)


def far(value):
    return pltpu.with_memory_space_constraint(value, pltpu.HBM)


def body(hidden_in, norm_gain, w_qkv, w_out, kv_cache, parents, lengths, assign):
    sections = lax.axis_size("section")
    ring = [(s, (s + 1) % sections) for s in range(sections)]
    pieces, state, table, gain, weight_in, cache = first(
        assign, parents, lengths, hidden_in, norm_gain, w_qkv, kv_cache
    )
    weights_in = (weight_in,)
    mates = [(t, t ^ 1) for t in range(pieces.shape[0])]
    for step in range(kv_cache.shape[1]):
        if step:
            pieces, sides = project(state, mine, come, gain, weights_in, step)
            spread = attend(exchange(pieces), table, cache, step, (sides,))
        else:
            spread = attend(exchange(pieces), table, cache, step)
        state, *mine = update(state, exchange(spread), w_out, step)
        if not step:
            weights_in += (rest(w_qkv, state),)
        state = lax.ppermute(state, "section", ring)
        if mine:
            (mine,) = mine
            come = lax.ppermute(mine, "tensor", mates)
    return state.reshape(hidden_in.shape)


def solution(mesh):
    in_specs = (
        P(("dp", "section"), None, None, "tensor"),
        P(("dp", "section"), None, "tensor"),
        P(("dp", "section"), None, "tensor", None),
        P(("dp", "section"), None, None, "tensor"),
        P(("dp", "section"), None, None, "tensor", None),
        P("dp", None),
        P("dp"),
        P("dp", None),
    )
    out_specs = P(("dp", "section"), None, None, "tensor")
    return jax.shard_map(body, mesh=mesh, in_specs=in_specs, out_specs=out_specs, check_vma=False)
```

```python
import functools

import jax
import jax.numpy as jnp
from jax import lax
from jax.experimental import pallas as pl
from jax.experimental.pallas import tpu as pltpu
from jax.sharding import PartitionSpec as P

bf16 = jnp.bfloat16
f32 = jnp.float32

D = 8192
epsilon = 1e-05
lowest = -1e30
largest = 3.3e38

TREE = 16
HEAD = 128
BOTH = 2 * HEAD
HALF = 512
MIX = 768
PIECE = 896
CHUNKS = 8
VMEM_LIMIT = 16 * 1024 * 1024

VMEM = pl.BlockSpec(memory_space=pltpu.VMEM)
FAR = pl.BlockSpec(memory_space=pltpu.HBM)
PARAMS = pltpu.CompilerParams(vmem_limit_bytes=VMEM_LIMIT)


def layer_of(step):
    return (lax.axis_index("section") < step).astype(jnp.int32)


def loads(source, target, sems):
    count = sems.shape[0]
    rows = target.shape[0] // count
    return [
        pltpu.make_async_copy(
            source.at[pl.ds(part * rows, rows), :],
            target.at[pl.ds(part * rows, rows), :],
            sems.at[part],
        )
        for part in range(count)
    ]


def write_pieces(out_ref, raw, state):
    square = jnp.sum(state * state, axis=-1, keepdims=True)
    high = jnp.minimum(square, largest).astype(bf16)
    low = (square - high.astype(f32)).astype(bf16)
    lane = lax.broadcasted_iota(jnp.int32, (state.shape[0], HEAD), 1)
    pair = jnp.where(lane < HEAD // 2, high.astype(f32), low.astype(f32)).astype(bf16)
    raw = raw.astype(bf16)
    for slot in range(out_ref.shape[0] // 2):
        here = slice(slot * TREE, (slot + 1) * TREE)
        for half in range(2):
            out_ref[2 * slot + half, :, :HALF] = raw[here, half * HALF : (half + 1) * HALF]
            out_ref[2 * slot + half, :, HALF:MIX] = raw[here, 2 * HALF :]
            out_ref[2 * slot + half, :, MIX:PIECE] = pair[here]


def chunks_of(cache_ref):
    return range(cache_ref.shape[2] // TREE)


def write_cache(out_ref, cache_ref, step, start):
    for slot in range(cache_ref.shape[1]):
        for chunk in chunks_of(cache_ref):
            block = cache_ref[step, slot, chunk * TREE : (chunk + 1) * TREE, :]
            place = start + chunk * BOTH
            for half in range(2):
                out_ref[2 * slot + half, :, place : place + BOTH] = block


def write_sides(out_ref, cache_ref, step, start):
    for slot in range(cache_ref.shape[1]):
        for chunk in chunks_of(cache_ref):
            here = slice(chunk * TREE, (chunk + 1) * TREE)
            place = start + chunk * HEAD
            for half in range(2):
                out_ref[2 * slot + half, :, place : place + HEAD] = cache_ref[
                    step, slot, here, half * HEAD : (half + 1) * HEAD
                ]


def first_kernel(
    assign_far, parents_far, lengths_far, state_far, gain_far, weight_far, cache_far,
    out_ref, state_ref, table_ref, gain_ref, weight_ref, cache_ref,
    assign_ref, parents_ref, lengths_ref, rows, sems, more,
):
    weight_copies = loads(weight_far.at[0, 0], weight_ref, sems)
    other = [
        pltpu.make_async_copy(source, target, more.at[index])
        for index, (source, target) in enumerate(
            (
                (assign_far, assign_ref),
                (parents_far, parents_ref),
                (lengths_far, lengths_ref),
                (state_far, state_ref),
                (gain_far.at[0], gain_ref),
                (cache_far.at[0], cache_ref),
            )
        )
    ]
    for copy in other[:5] + weight_copies + other[5:]:
        copy.start()
    for copy in other[:3]:
        copy.wait()
    batches = assign_ref.shape[1]
    section = lax.axis_index("section")
    slot = lax.axis_index("tensor") // 2
    lane = lax.broadcasted_iota(jnp.int32, (1, HEAD), 1)
    steps = range(table_ref.shape[0])
    held = [lax.rem(section - step + batches, batches) for step in steps]
    request = [assign_ref[slot, held[step]] for step in steps]
    for step in steps:
        rows[step, pl.ds(0, 1), :] = jnp.where(lane == 0, 1.0, 0.0)
    for node in range(1, TREE):
        parents = [parents_ref[node, request[step]] for step in steps]
        above = [rows[step, pl.ds(parents[step], 1), :] for step in steps]
        for step in steps:
            rows[step, pl.ds(node, 1), :] = jnp.where(lane == node, 1.0, above[step])
    for step in steps:
        live = lengths_ref[request[step]].astype(f32)
        table_ref[step] = jnp.where(lane < TREE, rows[step], live)
    other[3].wait()
    other[4].wait()
    width = state_ref.shape[1]
    state = state_ref[...]
    scaled = (state * gain_ref[0:1, :]).astype(bf16)
    depth = width // len(weight_copies)
    raw = jnp.zeros((state.shape[0], weight_ref.shape[1]), f32)
    for part, copy in enumerate(weight_copies):
        copy.wait()
        span = slice(part * depth, (part + 1) * depth)
        raw = raw + jnp.dot(scaled[:, span], weight_ref[span, :], preferred_element_type=f32)
    write_pieces(out_ref, raw, state)
    other[5].wait()
    write_cache(out_ref, cache_ref, 0, PIECE)


def first(assign, parents, lengths, hidden, gain, weight, cache):
    _, slots, tree, width = hidden.shape
    steps, _, span = cache.shape[1:4]
    rows = hidden.reshape(slots * tree, width)
    return pl.pallas_call(
        first_kernel,
        out_shape=(
            jax.ShapeDtypeStruct((2 * slots, TREE, PIECE + span // TREE * BOTH), bf16),
            pltpu.VMEM((slots * tree, width), f32),
            pltpu.VMEM((steps, TREE, HEAD), f32),
            pltpu.VMEM(gain.shape[1:], f32),
            pltpu.VMEM(weight.shape[2:], bf16),
            pltpu.VMEM(cache.shape[1:], bf16),
        ),
        in_specs=[FAR] * 7,
        out_specs=(VMEM,) * 6,
        scratch_shapes=[
            pltpu.SMEM(assign.shape[::-1], jnp.int32),
            pltpu.SMEM(parents.shape[::-1], jnp.int32),
            pltpu.SMEM(lengths.shape, jnp.int32),
            pltpu.VMEM((steps, TREE, HEAD), f32),
            pltpu.SemaphoreType.DMA((CHUNKS,)),
            pltpu.SemaphoreType.DMA((6,)),
        ],
        compiler_params=PARAMS,
    )(*map(far, (assign.T, parents.T, lengths, rows, gain, weight, cache)))


def rest_kernel(in_far, _, in_ref, sems):
    copies = loads(in_far.at[0, 1], in_ref, sems)
    for copy in copies:
        copy.start()
    for copy in copies:
        copy.wait()


def rest(weight_in, after):
    return pl.pallas_call(
        rest_kernel,
        out_shape=pltpu.VMEM(weight_in.shape[2:], bf16),
        in_specs=[FAR, VMEM],
        out_specs=VMEM,
        scratch_shapes=[pltpu.SemaphoreType.DMA((CHUNKS,))],
        compiler_params=PARAMS,
    )(far(weight_in), after)


def pick(step, act, layers):
    if len(layers) == 1:
        return act(layers[0])
    which = layer_of(step)
    for index, layer in enumerate(layers):
        pl.when(which == index)(functools.partial(act, layer))


def project_kernel(state_ref, gain_ref, *refs, step):
    *weight_refs, out_ref = refs
    state = state_ref[...]
    scaled = (state * gain_ref[pl.ds(layer_of(step), 1), :]).astype(bf16)

    def act(weight_ref):
        raw = jnp.dot(scaled, weight_ref[...], preferred_element_type=f32)
        write_pieces(out_ref, raw, state)

    pick(step, act, weight_refs)


def project(state, gain, weights, step):
    return pl.pallas_call(
        functools.partial(project_kernel, step=step),
        out_shape=jax.ShapeDtypeStruct((2 * state.shape[0] // TREE, TREE, PIECE), bf16),
        in_specs=[VMEM] * (2 + len(weights)),
        out_specs=VMEM,
        compiler_params=PARAMS,
    )(state, gain, *weights)


def attend_kernel(got_ref, table_ref, cache_ref, *refs, step):
    *sides_ref, out_ref = refs
    total = jnp.sum(got_ref[:, :, :PIECE].astype(f32), axis=0)
    square = total[:, MIX : MIX + 1] + total[:, MIX + HEAD // 2 : MIX + HEAD // 2 + 1]
    factor = lax.rsqrt(square / D + epsilon)
    projected = (total[:, :MIX] * factor).astype(bf16)
    heads = HALF // HEAD
    queries = jnp.concatenate(
        [projected[:, h * HEAD : (h + 1) * HEAD] for h in range(heads)], axis=0
    )
    tree_keys = projected[:, HALF : HALF + HEAD]
    tree_values = projected[:, HALF + HEAD :]
    if step:
        mine_ref, come_ref = sides_ref
        blocks = [
            [
                side_ref[piece, :, start : start + HEAD]
                for piece in range(side_ref.shape[0])
                for start in range(0, side_ref.shape[2], HEAD)
            ]
            for side_ref in (mine_ref, come_ref)
        ]
    else:
        blocks = [
            [
                got_ref[piece, :, start + side * HEAD : start + (side + 1) * HEAD]
                for piece in range(got_ref.shape[0])
                for start in range(PIECE, got_ref.shape[2], BOTH)
            ]
            for side in range(2)
        ]
    keys, values = (jnp.concatenate(block, axis=0) for block in blocks)
    if step:
        swapped = lax.rem(lax.axis_index("tensor"), 2) == 1
        keys, values = jnp.where(swapped, values, keys), jnp.where(swapped, keys, values)
    contract = (((1,), (1,)), ((), ()))
    scaling = HEAD ** (-0.5)
    scores = lax.dot_general(queries, keys, contract, preferred_element_type=f32)
    tree_scores = lax.dot_general(queries, tree_keys, contract, preferred_element_type=f32)
    position = lax.broadcasted_iota(jnp.int32, scores.shape, 1)
    table = table_ref[step]
    live = table[0:1, TREE : TREE + 1].astype(jnp.int32)
    visible = jnp.concatenate([table[:, :TREE]] * heads, axis=0) > 0.5
    scores = jnp.where(position < live, scores * scaling, lowest)
    tree_scores = jnp.where(visible, tree_scores * scaling, lowest)
    row_max = jnp.maximum(
        jnp.max(scores, axis=-1, keepdims=True), jnp.max(tree_scores, axis=-1, keepdims=True)
    )
    weights = jnp.exp(scores - row_max)
    tree_weights = jnp.exp(tree_scores - row_max)
    row_sum = jnp.sum(weights, axis=-1, keepdims=True) + jnp.sum(
        tree_weights, axis=-1, keepdims=True
    )
    weighted = jnp.dot(weights.astype(bf16), values, preferred_element_type=f32)
    weighted = weighted + jnp.dot(
        tree_weights.astype(bf16), tree_values, preferred_element_type=f32
    )
    attended = (weighted / row_sum).astype(bf16)
    for h in range(heads):
        part = attended[h * TREE : (h + 1) * TREE]
        for piece in range(out_ref.shape[0]):
            out_ref[piece, :, h * HEAD : (h + 1) * HEAD] = part
    if step + 1 < cache_ref.shape[0]:
        write_sides(out_ref, cache_ref, step + 1, HALF)


def attend(got, table, cache, step, sides=()):
    steps, _, span = cache.shape[:3]
    width = HALF + (span // TREE * HEAD if step + 1 < steps else 0)
    return pl.pallas_call(
        functools.partial(attend_kernel, step=step),
        out_shape=jax.ShapeDtypeStruct((got.shape[0], TREE, width), bf16),
        in_specs=[VMEM] * (3 + len(sides)),
        out_specs=VMEM,
        compiler_params=PARAMS,
    )(got, table, cache, *sides)


def update_kernel(state_ref, got_ref, weight_ref, *refs, step, last):
    if last:
        (out_ref,) = refs
    else:
        out_ref, side_ref = refs
        side_ref[...] = got_ref[:, :, HALF:]
    attended = jnp.concatenate(
        [
            jnp.concatenate([got_ref[at, :, :HALF], got_ref[at + 1, :, :HALF]], axis=1)
            for at in range(0, got_ref.shape[0], 2)
        ],
        axis=0,
    )

    delta = jnp.dot(attended, weight_ref[0, layer_of(step)], preferred_element_type=f32)
    out_ref[...] = state_ref[...] + delta


def update(state, got, weight, step):
    count, tree, total = got.shape
    out_shape = (jax.ShapeDtypeStruct(state.shape, f32),)
    last = total == HALF
    if not last:
        out_shape += (jax.ShapeDtypeStruct((count, tree, total - HALF), bf16),)
    return pl.pallas_call(
        functools.partial(update_kernel, step=step, last=last),
        out_shape=out_shape,
        in_specs=[VMEM] * 3,
        out_specs=(VMEM,) * len(out_shape),
        compiler_params=PARAMS,
    )(state, got, weight)


def exchange(value):
    return lax.all_to_all(value, "tensor", 0, 0, tiled=True)


def far(value):
    return pltpu.with_memory_space_constraint(value, pltpu.HBM)


def body(hidden_in, norm_gain, w_qkv, w_out, kv_cache, parents, lengths, assign):
    sections = lax.axis_size("section")
    ring = [(s, (s + 1) % sections) for s in range(sections)]
    pieces, state, table, gain, weight_in, cache = first(
        assign, parents, lengths, hidden_in, norm_gain, w_qkv, kv_cache
    )
    weights_in = (weight_in,)
    mates = [(t, t ^ 1) for t in range(pieces.shape[0])]
    for step in range(kv_cache.shape[1]):
        if step:
            pieces = project(state, gain, weights_in, step)
            pieces, come = lax.optimization_barrier((pieces, come))
            spread = attend(exchange(pieces), table, cache, step, (mine, come))
        else:
            spread = attend(exchange(pieces), table, cache, step)
        state, *mine = update(state, exchange(spread), w_out, step)
        if not step:
            weights_in += (rest(w_qkv, state),)
        state = lax.ppermute(state, "section", ring)
        if mine:
            (mine,) = mine
            come = lax.ppermute(mine, "tensor", mates)
    return state.reshape(hidden_in.shape)


def solution(mesh):
    in_specs = (
        P(("dp", "section"), None, None, "tensor"),
        P(("dp", "section"), None, "tensor"),
        P(("dp", "section"), None, "tensor", None),
        P(("dp", "section"), None, None, "tensor"),
        P(("dp", "section"), None, None, "tensor", None),
        P("dp", None),
        P("dp"),
        P("dp", None),
    )
    out_specs = P(("dp", "section"), None, None, "tensor")
    return jax.shard_map(body, mesh=mesh, in_specs=in_specs, out_specs=out_specs, check_vma=False)
```

```python
import functools

import jax
import jax.numpy as jnp
from jax import lax
from jax.experimental import pallas as pl
from jax.experimental.pallas import tpu as pltpu
from jax.sharding import PartitionSpec as P

bf16 = jnp.bfloat16
f32 = jnp.float32

D = 8192
epsilon = 1e-05
lowest = -1e30
largest = 3.3e38

TREE = 16
HEAD = 128
BOTH = 2 * HEAD
HALF = 512
MIX = 768
PIECE = 896
CHUNKS = 8
TOP = 125.0
PARTS = 1
VMEM_LIMIT = 16 * 1024 * 1024

VMEM = pl.BlockSpec(memory_space=pltpu.VMEM)
FAR = pl.BlockSpec(memory_space=pltpu.HBM)
PARAMS = pltpu.CompilerParams(vmem_limit_bytes=VMEM_LIMIT)


def layer_of(step):
    return (lax.axis_index("section") < step).astype(jnp.int32)


def loads(source, target, sems):
    count = sems.shape[0]
    rows = target.shape[0] // count
    return [
        pltpu.make_async_copy(
            source.at[pl.ds(part * rows, rows), :],
            target.at[pl.ds(part * rows, rows), :],
            sems.at[part],
        )
        for part in range(count)
    ]


def write_pieces(out_ref, raw, state):
    square = jnp.sum(state * state, axis=-1, keepdims=True)
    high = jnp.minimum(square, largest).astype(bf16)
    low = (square - high.astype(f32)).astype(bf16)
    lane = lax.broadcasted_iota(jnp.int32, (state.shape[0], HEAD), 1)
    pair = jnp.where(lane < HEAD // 2, high.astype(f32), low.astype(f32)).astype(bf16)
    raw = raw.astype(bf16)
    for slot in range(out_ref.shape[0] // 2):
        here = slice(slot * TREE, (slot + 1) * TREE)
        for half in range(2):
            out_ref[2 * slot + half, :, :HALF] = raw[here, half * HALF : (half + 1) * HALF]
            out_ref[2 * slot + half, :, HALF:MIX] = raw[here, 2 * HALF :]
            out_ref[2 * slot + half, :, MIX:PIECE] = pair[here]


def chunks_of(cache_ref):
    return range(cache_ref.shape[2] // TREE)


def write_cache(out_ref, cache_ref, step, start):
    for slot in range(cache_ref.shape[1]):
        for chunk in chunks_of(cache_ref):
            block = cache_ref[step, slot, chunk * TREE : (chunk + 1) * TREE, :]
            place = start + chunk * BOTH
            for half in range(2):
                out_ref[2 * slot + half, :, place : place + BOTH] = block


def write_sides(out_ref, cache_ref, step, start):
    for slot in range(cache_ref.shape[1]):
        for chunk in chunks_of(cache_ref):
            here = slice(chunk * TREE, (chunk + 1) * TREE)
            place = start + chunk * HEAD
            for half in range(2):
                out_ref[2 * slot + half, :, place : place + HEAD] = cache_ref[
                    step, slot, here, half * HEAD : (half + 1) * HEAD
                ]


def first_kernel(
    assign_far, parents_far, lengths_far, state_far, gain_far, weight_far, cache_far,
    out_ref, state_ref, table_ref, gain_ref, cache_ref,
    assign_ref, parents_ref, lengths_ref, rows, weight_ref, sems, more,
):
    weight_copies = loads(weight_far.at[0, 0], weight_ref, sems)
    other = [
        pltpu.make_async_copy(source, target, more.at[index])
        for index, (source, target) in enumerate(
            (
                (assign_far, assign_ref),
                (parents_far, parents_ref),
                (lengths_far, lengths_ref),
                (state_far, state_ref),
                (gain_far.at[0], gain_ref),
                (cache_far.at[0], cache_ref),
            )
        )
    ]
    for copy in other[:5] + weight_copies + other[5:]:
        copy.start()
    for copy in other[:3]:
        copy.wait()
    batches = assign_ref.shape[1]
    section = lax.axis_index("section")
    slot = lax.axis_index("tensor") // 2
    lane = lax.broadcasted_iota(jnp.int32, (1, HEAD), 1)
    steps = range(table_ref.shape[0])
    held = [lax.rem(section - step + batches, batches) for step in steps]
    request = [assign_ref[slot, held[step]] for step in steps]
    for step in steps:
        rows[step, pl.ds(0, 1), :] = jnp.where(lane == 0, 1.0, 0.0)
    for node in range(1, TREE):
        parents = [parents_ref[node, request[step]] for step in steps]
        above = [rows[step, pl.ds(parents[step], 1), :] for step in steps]
        for step in steps:
            rows[step, pl.ds(node, 1), :] = jnp.where(lane == node, 1.0, above[step])
    for step in steps:
        live = lengths_ref[request[step]].astype(f32)
        table_ref[step] = jnp.where(lane < TREE, rows[step], live)
    other[3].wait()
    other[4].wait()
    width = state_ref.shape[1]
    state = state_ref[...]
    scaled = (state * gain_ref[0:1, :]).astype(bf16)
    depth = width // len(weight_copies)
    raw = jnp.zeros((state.shape[0], weight_ref.shape[1]), f32)
    for part, copy in enumerate(weight_copies):
        copy.wait()
        span = slice(part * depth, (part + 1) * depth)
        raw = raw + jnp.dot(scaled[:, span], weight_ref[span, :], preferred_element_type=f32)
    write_pieces(out_ref, raw, state)
    other[5].wait()
    write_cache(out_ref, cache_ref, 0, PIECE)


def first(assign, parents, lengths, hidden, gain, weight, cache):
    _, slots, tree, width = hidden.shape
    steps, _, span = cache.shape[1:4]
    rows = hidden.reshape(slots * tree, width)
    return pl.pallas_call(
        first_kernel,
        out_shape=(
            jax.ShapeDtypeStruct((2 * slots, TREE, PIECE + span // TREE * BOTH), bf16),
            pltpu.VMEM((slots * tree, width), f32),
            pltpu.VMEM((steps, TREE, HEAD), f32),
            pltpu.VMEM(gain.shape[1:], f32),
            pltpu.VMEM(cache.shape[1:], bf16),
        ),
        in_specs=[FAR] * 7,
        out_specs=(VMEM,) * 5,
        scratch_shapes=[
            pltpu.SMEM(assign.shape[::-1], jnp.int32),
            pltpu.SMEM(parents.shape[::-1], jnp.int32),
            pltpu.SMEM(lengths.shape, jnp.int32),
            pltpu.VMEM((steps, TREE, HEAD), f32),
            pltpu.VMEM(weight.shape[2:], bf16),
            pltpu.SemaphoreType.DMA((CHUNKS,)),
            pltpu.SemaphoreType.DMA((6,)),
        ],
        compiler_params=PARAMS,
    )(*map(far, (assign.T, parents.T, lengths, rows, gain, weight, cache)))


def unit_of(power):
    return jnp.exp2(power) / jnp.where(power < TOP, 32767.0, 4095.0)


def pack(packed_ref, state):
    width = state.shape[1]
    peak = jnp.max(jnp.abs(state), axis=-1, keepdims=True)
    power = jnp.clip(jnp.ceil(jnp.log2(jnp.maximum(peak, 1e-37))), -TOP, TOP)
    ratio = state * jnp.exp2(-power) * jnp.where(power < TOP, 32767.0, 4095.0)
    steps = jnp.clip(jnp.round(ratio), -32767.0, 32767.0)
    packed_ref[:, :width] = steps.astype(jnp.int32).astype(jnp.int16)
    powers = jnp.broadcast_to(power.astype(jnp.int32), (state.shape[0], HEAD))
    packed_ref[:, width:] = powers.astype(jnp.int16)


def unpack(packed_ref):
    width = packed_ref.shape[1] - HEAD
    power = packed_ref[:, width:].astype(jnp.int32).astype(f32)[:, :1]
    return packed_ref[:, :width].astype(jnp.int32).astype(f32) * unit_of(power)


def expand_kernel(*refs):
    *packed_refs, out_ref = refs
    out_ref[...] = jnp.concatenate([unpack(packed_ref) for packed_ref in packed_refs], axis=0)


def expand(packed):
    rows, width = packed[0].shape
    return pl.pallas_call(
        expand_kernel,
        out_shape=jax.ShapeDtypeStruct((rows * len(packed), width - HEAD), f32),
        in_specs=[VMEM] * len(packed),
        out_specs=VMEM,
        compiler_params=PARAMS,
    )(*packed)


def project_kernel(*refs, step):
    *packed_refs, gain_ref, weight_ref, out_ref, state_ref = refs
    state = jnp.concatenate([unpack(packed_ref) for packed_ref in packed_refs], axis=0)
    state_ref[...] = state
    which = layer_of(step)
    scaled = (state * gain_ref[pl.ds(which, 1), :]).astype(bf16)
    raw = jnp.dot(scaled, weight_ref[0, which], preferred_element_type=f32)
    write_pieces(out_ref, raw, state)


def project(packed, gain, weight, step):
    rows, width = packed[0].shape
    rows *= len(packed)
    return pl.pallas_call(
        functools.partial(project_kernel, step=step),
        out_shape=(
            jax.ShapeDtypeStruct((2 * rows // TREE, TREE, PIECE), bf16),
            jax.ShapeDtypeStruct((rows, width - HEAD), f32),
        ),
        in_specs=[VMEM] * (2 + len(packed)),
        out_specs=(VMEM,) * 2,
        compiler_params=PARAMS,
    )(*packed, gain, weight)


def attend_kernel(got_ref, table_ref, cache_ref, *refs, step):
    *sides_ref, out_ref = refs
    total = jnp.sum(got_ref[:, :, :PIECE].astype(f32), axis=0)
    square = total[:, MIX : MIX + 1] + total[:, MIX + HEAD // 2 : MIX + HEAD // 2 + 1]
    factor = lax.rsqrt(square / D + epsilon)
    projected = (total[:, :MIX] * factor).astype(bf16)
    heads = HALF // HEAD
    queries = jnp.concatenate(
        [projected[:, h * HEAD : (h + 1) * HEAD] for h in range(heads)], axis=0
    )
    tree_keys = projected[:, HALF : HALF + HEAD]
    tree_values = projected[:, HALF + HEAD :]
    if step:
        mine_ref, come_ref = sides_ref
        blocks = [
            [
                side_ref[piece, :, start : start + HEAD]
                for piece in range(side_ref.shape[0])
                for start in range(0, side_ref.shape[2], HEAD)
            ]
            for side_ref in (mine_ref, come_ref)
        ]
    else:
        blocks = [
            [
                got_ref[piece, :, start + side * HEAD : start + (side + 1) * HEAD]
                for piece in range(got_ref.shape[0])
                for start in range(PIECE, got_ref.shape[2], BOTH)
            ]
            for side in range(2)
        ]
    keys, values = (jnp.concatenate(block, axis=0) for block in blocks)
    if step:
        swapped = lax.rem(lax.axis_index("tensor"), 2) == 1
        keys, values = jnp.where(swapped, values, keys), jnp.where(swapped, keys, values)
    contract = (((1,), (1,)), ((), ()))
    scaling = HEAD ** (-0.5)
    scores = lax.dot_general(queries, keys, contract, preferred_element_type=f32)
    tree_scores = lax.dot_general(queries, tree_keys, contract, preferred_element_type=f32)
    position = lax.broadcasted_iota(jnp.int32, scores.shape, 1)
    table = table_ref[step]
    live = table[0:1, TREE : TREE + 1].astype(jnp.int32)
    visible = jnp.concatenate([table[:, :TREE]] * heads, axis=0) > 0.5
    scores = jnp.where(position < live, scores * scaling, lowest)
    tree_scores = jnp.where(visible, tree_scores * scaling, lowest)
    row_max = jnp.maximum(
        jnp.max(scores, axis=-1, keepdims=True), jnp.max(tree_scores, axis=-1, keepdims=True)
    )
    weights = jnp.exp(scores - row_max)
    tree_weights = jnp.exp(tree_scores - row_max)
    row_sum = jnp.sum(weights, axis=-1, keepdims=True) + jnp.sum(
        tree_weights, axis=-1, keepdims=True
    )
    weighted = jnp.dot(weights.astype(bf16), values, preferred_element_type=f32)
    weighted = weighted + jnp.dot(
        tree_weights.astype(bf16), tree_values, preferred_element_type=f32
    )
    attended = (weighted / row_sum).astype(bf16)
    for h in range(heads):
        part = attended[h * TREE : (h + 1) * TREE]
        for piece in range(out_ref.shape[0]):
            out_ref[piece, :, h * HEAD : (h + 1) * HEAD] = part
    if step + 1 < cache_ref.shape[0]:
        write_sides(out_ref, cache_ref, step + 1, HALF)


def attend(got, table, cache, step, sides=()):
    steps, _, span = cache.shape[:3]
    width = HALF + (span // TREE * HEAD if step + 1 < steps else 0)
    return pl.pallas_call(
        functools.partial(attend_kernel, step=step),
        out_shape=jax.ShapeDtypeStruct((got.shape[0], TREE, width), bf16),
        in_specs=[VMEM] * (3 + len(sides)),
        out_specs=VMEM,
        compiler_params=PARAMS,
    )(got, table, cache, *sides)


def update_kernel(state_ref, got_ref, weight_ref, *refs, step, last):
    if last:
        out_refs = refs
    else:
        *out_refs, side_ref = refs
        side_ref[...] = got_ref[:, :, HALF:]
    attended = jnp.concatenate(
        [
            jnp.concatenate([got_ref[at, :, :HALF], got_ref[at + 1, :, :HALF]], axis=1)
            for at in range(0, got_ref.shape[0], 2)
        ],
        axis=0,
    )

    delta = jnp.dot(attended, weight_ref[0, layer_of(step)], preferred_element_type=f32)
    state = state_ref[...] + delta
    rows = out_refs[0].shape[0]
    for part, out_ref in enumerate(out_refs):
        pack(out_ref, state[part * rows : (part + 1) * rows])


def update(state, got, weight, step):
    rows, width = state.shape
    count, tree, total = got.shape
    out_shape = (jax.ShapeDtypeStruct((rows // PARTS, width + HEAD), jnp.int16),) * PARTS
    last = total == HALF
    if not last:
        out_shape += (jax.ShapeDtypeStruct((count, tree, total - HALF), bf16),)
    return pl.pallas_call(
        functools.partial(update_kernel, step=step, last=last),
        out_shape=out_shape,
        in_specs=[VMEM] * 3,
        out_specs=(VMEM,) * len(out_shape),
        compiler_params=PARAMS,
    )(state, got, weight)


def exchange(value):
    return lax.all_to_all(value, "tensor", 0, 0, tiled=True)


def far(value):
    return pltpu.with_memory_space_constraint(value, pltpu.HBM)


def body(hidden_in, norm_gain, w_qkv, w_out, kv_cache, parents, lengths, assign):
    sections = lax.axis_size("section")
    ring = [(s, (s + 1) % sections) for s in range(sections)]
    pieces, state, table, gain, cache = first(
        assign, parents, lengths, hidden_in, norm_gain, w_qkv, kv_cache
    )
    mates = [(t, t ^ 1) for t in range(pieces.shape[0])]
    for step in range(kv_cache.shape[1]):
        if step:
            pieces, state = project(packed, gain, w_qkv, step)
            pieces, come = lax.optimization_barrier((pieces, come))
            spread = attend(exchange(pieces), table, cache, step, (mine, come))
        else:
            spread = attend(exchange(pieces), table, cache, step)
        outs = update(state, exchange(spread), w_out, step)
        parts = [lax.ppermute(part, "section", ring) for part in jnp.split(outs[0], [48])]
        packed = [jnp.concatenate(parts)]
        if len(outs) > 1:
            mine = outs[1]
            come = lax.ppermute(mine, "tensor", mates)
    return expand(packed).reshape(hidden_in.shape)


def solution(mesh):
    in_specs = (
        P(("dp", "section"), None, None, "tensor"),
        P(("dp", "section"), None, "tensor"),
        P(("dp", "section"), None, "tensor", None),
        P(("dp", "section"), None, None, "tensor"),
        P(("dp", "section"), None, None, "tensor", None),
        P("dp", None),
        P("dp"),
        P("dp", None),
    )
    out_specs = P(("dp", "section"), None, None, "tensor")
    return jax.shard_map(body, mesh=mesh, in_specs=in_specs, out_specs=out_specs, check_vma=False)
```

```python
import functools

import jax
import jax.numpy as jnp
from jax import lax
from jax.experimental import pallas as pl
from jax.experimental.pallas import tpu as pltpu
from jax.sharding import PartitionSpec as P

bf16 = jnp.bfloat16
f32 = jnp.float32

D = 8192
epsilon = 1e-05
lowest = -1e30
largest = 3.3e38

TREE = 16
HEAD = 128
BOTH = 2 * HEAD
HALF = 512
MIX = 768
PIECE = 896
CHUNKS = 8
TOP = 125.0
VMEM_LIMIT = 16 * 1024 * 1024

VMEM = pl.BlockSpec(memory_space=pltpu.VMEM)
FAR = pl.BlockSpec(memory_space=pltpu.HBM)
PARAMS = pltpu.CompilerParams(vmem_limit_bytes=VMEM_LIMIT)


def layer_of(step):
    return (lax.axis_index("section") < step).astype(jnp.int32)


def loads(source, target, sems):
    count = sems.shape[0]
    rows = target.shape[0] // count
    return [
        pltpu.make_async_copy(
            source.at[pl.ds(part * rows, rows), :],
            target.at[pl.ds(part * rows, rows), :],
            sems.at[part],
        )
        for part in range(count)
    ]


def write_pieces(out_ref, raw, state):
    square = jnp.sum(state * state, axis=-1, keepdims=True)
    high = jnp.minimum(square, largest).astype(bf16)
    low = (square - high.astype(f32)).astype(bf16)
    lane = lax.broadcasted_iota(jnp.int32, (state.shape[0], HEAD), 1)
    pair = jnp.where(lane < HEAD // 2, high.astype(f32), low.astype(f32)).astype(bf16)
    raw = raw.astype(bf16)
    for slot in range(out_ref.shape[0] // 2):
        here = slice(slot * TREE, (slot + 1) * TREE)
        for half in range(2):
            out_ref[2 * slot + half, :, :HALF] = raw[here, half * HALF : (half + 1) * HALF]
            out_ref[2 * slot + half, :, HALF:MIX] = raw[here, 2 * HALF :]
            out_ref[2 * slot + half, :, MIX:PIECE] = pair[here]


def chunks_of(cache_ref):
    return range(cache_ref.shape[2] // TREE)


def write_cache(out_ref, cache_ref, step, start):
    for slot in range(cache_ref.shape[1]):
        for chunk in chunks_of(cache_ref):
            block = cache_ref[step, slot, chunk * TREE : (chunk + 1) * TREE, :]
            place = start + chunk * BOTH
            for half in range(2):
                out_ref[2 * slot + half, :, place : place + BOTH] = block


def write_sides(out_ref, cache_ref, step, start):
    for slot in range(cache_ref.shape[1]):
        for chunk in chunks_of(cache_ref):
            here = slice(chunk * TREE, (chunk + 1) * TREE)
            place = start + chunk * HEAD
            for half in range(2):
                out_ref[2 * slot + half, :, place : place + HEAD] = cache_ref[
                    step, slot, here, half * HEAD : (half + 1) * HEAD
                ]


def first_kernel(
    assign_far, parents_far, lengths_far, state_far, gain_far, weight_far, cache_far,
    out_ref, state_ref, table_ref, gain_ref, cache_ref,
    assign_ref, parents_ref, lengths_ref, rows, weight_ref, sems, more,
):
    weight_copies = loads(weight_far.at[0, 0], weight_ref, sems)
    other = [
        pltpu.make_async_copy(source, target, more.at[index])
        for index, (source, target) in enumerate(
            (
                (assign_far, assign_ref),
                (parents_far, parents_ref),
                (lengths_far, lengths_ref),
                (state_far, state_ref),
                (gain_far.at[0], gain_ref),
                (cache_far.at[0], cache_ref),
            )
        )
    ]
    for copy in other[:5] + weight_copies + other[5:]:
        copy.start()
    for copy in other[:3]:
        copy.wait()
    batches = assign_ref.shape[1]
    section = lax.axis_index("section")
    slot = lax.axis_index("tensor") // 2
    lane = lax.broadcasted_iota(jnp.int32, (1, HEAD), 1)
    steps = range(table_ref.shape[0])
    held = [lax.rem(section - step + batches, batches) for step in steps]
    request = [assign_ref[slot, held[step]] for step in steps]
    for step in steps:
        rows[step, pl.ds(0, 1), :] = jnp.where(lane == 0, 1.0, 0.0)
    for node in range(1, TREE):
        parents = [parents_ref[node, request[step]] for step in steps]
        above = [rows[step, pl.ds(parents[step], 1), :] for step in steps]
        for step in steps:
            rows[step, pl.ds(node, 1), :] = jnp.where(lane == node, 1.0, above[step])
    for step in steps:
        live = lengths_ref[request[step]].astype(f32)
        table_ref[step] = jnp.where(lane < TREE, rows[step], live)
    other[3].wait()
    other[4].wait()
    width = state_ref.shape[1]
    state = state_ref[...]
    scaled = (state * gain_ref[0:1, :]).astype(bf16)
    depth = width // len(weight_copies)
    raw = jnp.zeros((state.shape[0], weight_ref.shape[1]), f32)
    for part, copy in enumerate(weight_copies):
        copy.wait()
        span = slice(part * depth, (part + 1) * depth)
        raw = raw + jnp.dot(scaled[:, span], weight_ref[span, :], preferred_element_type=f32)
    write_pieces(out_ref, raw, state)
    other[5].wait()
    write_cache(out_ref, cache_ref, 0, PIECE)


def first(assign, parents, lengths, hidden, gain, weight, cache):
    _, slots, tree, width = hidden.shape
    steps, _, span = cache.shape[1:4]
    rows = hidden.reshape(slots * tree, width)
    return pl.pallas_call(
        first_kernel,
        out_shape=(
            jax.ShapeDtypeStruct((2 * slots, TREE, PIECE + span // TREE * BOTH), bf16),
            pltpu.VMEM((slots * tree, width), f32),
            pltpu.VMEM((steps, TREE, HEAD), f32),
            pltpu.VMEM(gain.shape[1:], f32),
            pltpu.VMEM(cache.shape[1:], bf16),
        ),
        in_specs=[FAR] * 7,
        out_specs=(VMEM,) * 5,
        scratch_shapes=[
            pltpu.SMEM(assign.shape[::-1], jnp.int32),
            pltpu.SMEM(parents.shape[::-1], jnp.int32),
            pltpu.SMEM(lengths.shape, jnp.int32),
            pltpu.VMEM((steps, TREE, HEAD), f32),
            pltpu.VMEM(weight.shape[2:], bf16),
            pltpu.SemaphoreType.DMA((CHUNKS,)),
            pltpu.SemaphoreType.DMA((6,)),
        ],
        compiler_params=PARAMS,
    )(*map(far, (assign.T, parents.T, lengths, rows, gain, weight, cache)))


def unit_of(power):
    return jnp.exp2(power) / jnp.where(power < TOP, 32767.0, 4095.0)


def pack(early_ref, late_ref, state):
    width = state.shape[1]
    peak = jnp.max(jnp.abs(state), axis=-1, keepdims=True)
    power = jnp.clip(jnp.ceil(jnp.log2(jnp.maximum(peak, 1e-37))), -TOP, TOP)
    ratio = state * jnp.exp2(-power) * jnp.where(power < TOP, 32767.0, 4095.0)
    steps = jnp.clip(jnp.round(ratio), -32767.0, 32767.0).astype(jnp.int32).astype(jnp.int16)
    rows = early_ref.shape[0]
    early_ref[...] = steps[:rows]
    late_ref[:, :width] = steps[rows:]
    slots = state.shape[0] // TREE
    lane = lax.broadcasted_iota(jnp.int32, (TREE, HEAD), 1)
    powers = jnp.zeros((TREE, HEAD), f32)
    for slot in range(slots):
        mine = power[slot * TREE : (slot + 1) * TREE]
        powers = jnp.where(lane >= slot * (HEAD // slots), mine, powers)
    late_ref[:, width:] = powers.astype(jnp.int32).astype(jnp.int16)


def unpack(steps_ref, powers_ref):
    slots = steps_ref.shape[0] // TREE
    powers = powers_ref[...].astype(jnp.int32).astype(f32)
    gap = HEAD // slots
    power = jnp.concatenate(
        [powers[:, slot * gap : slot * gap + 1] for slot in range(slots)], axis=0
    )
    return steps_ref[...].astype(jnp.int32).astype(f32) * unit_of(power)


def expand_kernel(steps_ref, powers_ref, out_ref):
    out_ref[...] = unpack(steps_ref, powers_ref)


def expand(packed):
    return pl.pallas_call(
        expand_kernel,
        out_shape=jax.ShapeDtypeStruct(packed[0].shape, f32),
        in_specs=[VMEM] * 2,
        out_specs=VMEM,
        compiler_params=PARAMS,
    )(*packed)


def project_kernel(*refs, step):
    steps_ref, powers_ref, gain_ref, weight_ref, out_ref, state_ref = refs
    state = unpack(steps_ref, powers_ref)
    state_ref[...] = state
    which = layer_of(step)
    scaled = (state * gain_ref[pl.ds(which, 1), :]).astype(bf16)
    raw = jnp.dot(scaled, weight_ref[0, which], preferred_element_type=f32)
    write_pieces(out_ref, raw, state)


def project(packed, gain, weight, step):
    rows, width = packed[0].shape
    return pl.pallas_call(
        functools.partial(project_kernel, step=step),
        out_shape=(
            jax.ShapeDtypeStruct((2 * rows // TREE, TREE, PIECE), bf16),
            jax.ShapeDtypeStruct((rows, width), f32),
        ),
        in_specs=[VMEM] * (2 + len(packed)),
        out_specs=(VMEM,) * 2,
        compiler_params=PARAMS,
    )(*packed, gain, weight)


def attend_kernel(got_ref, table_ref, cache_ref, *refs, step):
    *sides_ref, out_ref = refs
    total = jnp.sum(got_ref[:, :, :PIECE].astype(f32), axis=0)
    square = total[:, MIX : MIX + 1] + total[:, MIX + HEAD // 2 : MIX + HEAD // 2 + 1]
    factor = lax.rsqrt(square / D + epsilon)
    projected = (total[:, :MIX] * factor).astype(bf16)
    heads = HALF // HEAD
    queries = jnp.concatenate(
        [projected[:, h * HEAD : (h + 1) * HEAD] for h in range(heads)], axis=0
    )
    tree_keys = projected[:, HALF : HALF + HEAD]
    tree_values = projected[:, HALF + HEAD :]
    if step:
        mine_ref, come_ref = sides_ref
        blocks = [
            [
                side_ref[piece, :, start : start + HEAD]
                for piece in range(side_ref.shape[0])
                for start in range(0, side_ref.shape[2], HEAD)
            ]
            for side_ref in (mine_ref, come_ref)
        ]
    else:
        blocks = [
            [
                got_ref[piece, :, start + side * HEAD : start + (side + 1) * HEAD]
                for piece in range(got_ref.shape[0])
                for start in range(PIECE, got_ref.shape[2], BOTH)
            ]
            for side in range(2)
        ]
    keys, values = (jnp.concatenate(block, axis=0) for block in blocks)
    if step:
        swapped = lax.rem(lax.axis_index("tensor"), 2) == 1
        keys, values = jnp.where(swapped, values, keys), jnp.where(swapped, keys, values)
    contract = (((1,), (1,)), ((), ()))
    scaling = HEAD ** (-0.5)
    scores = lax.dot_general(queries, keys, contract, preferred_element_type=f32)
    tree_scores = lax.dot_general(queries, tree_keys, contract, preferred_element_type=f32)
    position = lax.broadcasted_iota(jnp.int32, scores.shape, 1)
    table = table_ref[step]
    live = table[0:1, TREE : TREE + 1].astype(jnp.int32)
    visible = jnp.concatenate([table[:, :TREE]] * heads, axis=0) > 0.5
    scores = jnp.where(position < live, scores * scaling, lowest)
    tree_scores = jnp.where(visible, tree_scores * scaling, lowest)
    row_max = jnp.maximum(
        jnp.max(scores, axis=-1, keepdims=True), jnp.max(tree_scores, axis=-1, keepdims=True)
    )
    weights = jnp.exp(scores - row_max)
    tree_weights = jnp.exp(tree_scores - row_max)
    row_sum = jnp.sum(weights, axis=-1, keepdims=True) + jnp.sum(
        tree_weights, axis=-1, keepdims=True
    )
    weighted = jnp.dot(weights.astype(bf16), values, preferred_element_type=f32)
    weighted = weighted + jnp.dot(
        tree_weights.astype(bf16), tree_values, preferred_element_type=f32
    )
    attended = (weighted / row_sum).astype(bf16)
    for h in range(heads):
        part = attended[h * TREE : (h + 1) * TREE]
        for piece in range(out_ref.shape[0]):
            out_ref[piece, :, h * HEAD : (h + 1) * HEAD] = part
    if step + 1 < cache_ref.shape[0]:
        write_sides(out_ref, cache_ref, step + 1, HALF)


def attend(got, table, cache, step, sides=()):
    steps, _, span = cache.shape[:3]
    width = HALF + (span // TREE * HEAD if step + 1 < steps else 0)
    return pl.pallas_call(
        functools.partial(attend_kernel, step=step),
        out_shape=jax.ShapeDtypeStruct((got.shape[0], TREE, width), bf16),
        in_specs=[VMEM] * (3 + len(sides)),
        out_specs=VMEM,
        compiler_params=PARAMS,
    )(got, table, cache, *sides)


def update_kernel(state_ref, got_ref, weight_ref, *refs, step, last):
    if last:
        out_refs = refs
    else:
        *out_refs, side_ref = refs
        side_ref[...] = got_ref[:, :, HALF:]
    attended = jnp.concatenate(
        [
            jnp.concatenate([got_ref[at, :, :HALF], got_ref[at + 1, :, :HALF]], axis=1)
            for at in range(0, got_ref.shape[0], 2)
        ],
        axis=0,
    )

    delta = jnp.dot(attended, weight_ref[0, layer_of(step)], preferred_element_type=f32)
    pack(*out_refs, state_ref[...] + delta)


def update(state, got, weight, step):
    rows, width = state.shape
    count, tree, total = got.shape
    out_shape = (
        jax.ShapeDtypeStruct((rows - TREE, width), jnp.int16),
        jax.ShapeDtypeStruct((TREE, width + HEAD), jnp.int16),
    )
    last = total == HALF
    if not last:
        out_shape += (jax.ShapeDtypeStruct((count, tree, total - HALF), bf16),)
    return pl.pallas_call(
        functools.partial(update_kernel, step=step, last=last),
        out_shape=out_shape,
        in_specs=[VMEM] * 3,
        out_specs=(VMEM,) * len(out_shape),
        compiler_params=PARAMS,
    )(state, got, weight)


def exchange(value):
    return lax.all_to_all(value, "tensor", 0, 0, tiled=True)


def far(value):
    return pltpu.with_memory_space_constraint(value, pltpu.HBM)


def body(hidden_in, norm_gain, w_qkv, w_out, kv_cache, parents, lengths, assign):
    sections = lax.axis_size("section")
    ring = [(s, (s + 1) % sections) for s in range(sections)]
    pieces, state, table, gain, cache = first(
        assign, parents, lengths, hidden_in, norm_gain, w_qkv, kv_cache
    )
    mates = [(t, t ^ 1) for t in range(pieces.shape[0])]
    for step in range(kv_cache.shape[1]):
        if step:
            pieces, state = project(packed, gain, w_qkv, step)
            pieces, come = lax.optimization_barrier((pieces, come))
            spread = attend(exchange(pieces), table, cache, step, (mine, come))
        else:
            spread = attend(exchange(pieces), table, cache, step)
        outs = update(state, exchange(spread), w_out, step)
        early, late = (lax.ppermute(part, "section", ring) for part in outs[:2])
        width = early.shape[1]
        packed = (jnp.concatenate([early, late[:, :width]]), late[:, width:])
        if len(outs) > 2:
            mine = outs[2]
            come = lax.ppermute(mine, "tensor", mates)
    return expand(packed).reshape(hidden_in.shape)


def solution(mesh):
    in_specs = (
        P(("dp", "section"), None, None, "tensor"),
        P(("dp", "section"), None, "tensor"),
        P(("dp", "section"), None, "tensor", None),
        P(("dp", "section"), None, None, "tensor"),
        P(("dp", "section"), None, None, "tensor", None),
        P("dp", None),
        P("dp"),
        P("dp", None),
    )
    out_specs = P(("dp", "section"), None, None, "tensor")
    return jax.shard_map(body, mesh=mesh, in_specs=in_specs, out_specs=out_specs, check_vma=False)
```

```python
import functools

import jax
import jax.numpy as jnp
from jax import lax
from jax.experimental import pallas as pl
from jax.experimental.pallas import tpu as pltpu
from jax.sharding import PartitionSpec as P

bf16 = jnp.bfloat16
f32 = jnp.float32

D = 8192
epsilon = 1e-05
lowest = -1e30
largest = 3.3e38

TREE = 16
HEAD = 128
BOTH = 2 * HEAD
HALF = 512
MIX = 768
PIECE = 896
CHUNKS = 4
TOP = 125.0
VMEM_LIMIT = 16 * 1024 * 1024

VMEM = pl.BlockSpec(memory_space=pltpu.VMEM)
FAR = pl.BlockSpec(memory_space=pltpu.HBM)
PARAMS = pltpu.CompilerParams(vmem_limit_bytes=VMEM_LIMIT)


def layer_of(step):
    return (lax.axis_index("section") < step).astype(jnp.int32)


def loads(source, target, sems):
    count = sems.shape[0]
    rows = target.shape[0] // count
    return [
        pltpu.make_async_copy(
            source.at[pl.ds(part * rows, rows), :],
            target.at[pl.ds(part * rows, rows), :],
            sems.at[part],
        )
        for part in range(count)
    ]


def write_pieces(out_ref, raw, state):
    square = jnp.sum(state * state, axis=-1, keepdims=True)
    high = jnp.minimum(square, largest).astype(bf16)
    low = (square - high.astype(f32)).astype(bf16)
    lane = lax.broadcasted_iota(jnp.int32, (state.shape[0], HEAD), 1)
    pair = jnp.where(lane < HEAD // 2, high.astype(f32), low.astype(f32)).astype(bf16)
    raw = raw.astype(bf16)
    for slot in range(out_ref.shape[0] // 2):
        here = slice(slot * TREE, (slot + 1) * TREE)
        for half in range(2):
            out_ref[2 * slot + half, :, :HALF] = raw[here, half * HALF : (half + 1) * HALF]
            out_ref[2 * slot + half, :, HALF:MIX] = raw[here, 2 * HALF :]
            out_ref[2 * slot + half, :, MIX:PIECE] = pair[here]


def chunks_of(cache_ref):
    return range(cache_ref.shape[2] // TREE)


def write_cache(out_ref, cache_ref, step, start):
    for slot in range(cache_ref.shape[1]):
        for chunk in chunks_of(cache_ref):
            block = cache_ref[step, slot, chunk * TREE : (chunk + 1) * TREE, :]
            place = start + chunk * BOTH
            for half in range(2):
                out_ref[2 * slot + half, :, place : place + BOTH] = block


def write_sides(out_ref, cache_ref, step, start):
    for slot in range(cache_ref.shape[1]):
        for chunk in chunks_of(cache_ref):
            here = slice(chunk * TREE, (chunk + 1) * TREE)
            place = start + chunk * HEAD
            for half in range(2):
                out_ref[2 * slot + half, :, place : place + HEAD] = cache_ref[
                    step, slot, here, half * HEAD : (half + 1) * HEAD
                ]


def first_kernel(
    assign_far, parents_far, lengths_far, state_far, gain_far, weight_far, cache_far,
    out_ref, state_ref, table_ref, gain_ref,
    assign_ref, parents_ref, lengths_ref, rows, weight_ref, cache_ref, sems, more,
):
    weight_copies = loads(weight_far.at[0, 0], weight_ref, sems)
    other = [
        pltpu.make_async_copy(source, target, more.at[index])
        for index, (source, target) in enumerate(
            (
                (assign_far, assign_ref),
                (parents_far, parents_ref),
                (lengths_far, lengths_ref),
                (state_far, state_ref),
                (gain_far.at[0], gain_ref),
                (cache_far.at[0, pl.ds(0, 1)], cache_ref),
            )
        )
    ]
    for copy in other[:5] + weight_copies + other[5:]:
        copy.start()
    for copy in other[:3]:
        copy.wait()
    batches = assign_ref.shape[1]
    section = lax.axis_index("section")
    slot = lax.axis_index("tensor") // 2
    lane = lax.broadcasted_iota(jnp.int32, (1, HEAD), 1)
    steps = range(table_ref.shape[0])
    held = [lax.rem(section - step + batches, batches) for step in steps]
    request = [assign_ref[slot, held[step]] for step in steps]
    for step in steps:
        rows[step, pl.ds(0, 1), :] = jnp.where(lane == 0, 1.0, 0.0)
    for node in range(1, TREE):
        parents = [parents_ref[node, request[step]] for step in steps]
        above = [rows[step, pl.ds(parents[step], 1), :] for step in steps]
        for step in steps:
            rows[step, pl.ds(node, 1), :] = jnp.where(lane == node, 1.0, above[step])
    for step in steps:
        live = lengths_ref[request[step]].astype(f32)
        table_ref[step] = jnp.where(lane < TREE, rows[step], live)
    other[3].wait()
    other[4].wait()
    width = state_ref.shape[1]
    state = state_ref[...]
    scaled = (state * gain_ref[0:1, :]).astype(bf16)
    depth = width // len(weight_copies)
    raw = jnp.zeros((state.shape[0], weight_ref.shape[1]), f32)
    for part, copy in enumerate(weight_copies):
        copy.wait()
        span = slice(part * depth, (part + 1) * depth)
        raw = raw + jnp.dot(scaled[:, span], weight_ref[span, :], preferred_element_type=f32)
    write_pieces(out_ref, raw, state)
    other[5].wait()
    write_cache(out_ref, cache_ref, 0, PIECE)


def first(assign, parents, lengths, hidden, gain, weight, cache):
    _, slots, tree, width = hidden.shape
    steps, _, span = cache.shape[1:4]
    rows = hidden.reshape(slots * tree, width)
    return pl.pallas_call(
        first_kernel,
        out_shape=(
            jax.ShapeDtypeStruct((2 * slots, TREE, PIECE + span // TREE * BOTH), bf16),
            pltpu.VMEM((slots * tree, width), f32),
            pltpu.VMEM((steps, TREE, HEAD), f32),
            pltpu.VMEM(gain.shape[1:], f32),
        ),
        in_specs=[FAR] * 7,
        out_specs=(VMEM,) * 4,
        scratch_shapes=[
            pltpu.SMEM(assign.shape[::-1], jnp.int32),
            pltpu.SMEM(parents.shape[::-1], jnp.int32),
            pltpu.SMEM(lengths.shape, jnp.int32),
            pltpu.VMEM((steps, TREE, HEAD), f32),
            pltpu.VMEM(weight.shape[2:], bf16),
            pltpu.VMEM((1,) + cache.shape[2:], bf16),
            pltpu.SemaphoreType.DMA((CHUNKS,)),
            pltpu.SemaphoreType.DMA((6,)),
        ],
        compiler_params=PARAMS,
    )(*map(far, (assign.T, parents.T, lengths, rows, gain, weight, cache)))


def unit_of(power):
    return jnp.exp2(power) / jnp.where(power < TOP, 32767.0, 4095.0)


def pack(early_ref, late_ref, state):
    width = state.shape[1]
    peak = jnp.max(jnp.abs(state), axis=-1, keepdims=True)
    power = jnp.clip(jnp.ceil(jnp.log2(jnp.maximum(peak, 1e-37))), -TOP, TOP)
    ratio = state * jnp.exp2(-power) * jnp.where(power < TOP, 32767.0, 4095.0)
    steps = jnp.clip(jnp.round(ratio), -32767.0, 32767.0).astype(jnp.int32).astype(jnp.int16)
    rows = early_ref.shape[0]
    early_ref[...] = steps[:rows]
    late_ref[:, :width] = steps[rows:]
    slots = state.shape[0] // TREE
    lane = lax.broadcasted_iota(jnp.int32, (TREE, HEAD), 1)
    powers = jnp.zeros((TREE, HEAD), f32)
    for slot in range(slots):
        mine = power[slot * TREE : (slot + 1) * TREE]
        powers = jnp.where(lane >= slot * (HEAD // slots), mine, powers)
    late_ref[:, width:] = powers.astype(jnp.int32).astype(jnp.int16)


def unpack(steps_ref, powers_ref):
    slots = steps_ref.shape[0] // TREE
    powers = powers_ref[...].astype(jnp.int32).astype(f32)
    gap = HEAD // slots
    power = jnp.concatenate(
        [powers[:, slot * gap : slot * gap + 1] for slot in range(slots)], axis=0
    )
    return steps_ref[...].astype(jnp.int32).astype(f32) * unit_of(power)


def expand_kernel(steps_ref, powers_ref, out_ref):
    out_ref[...] = unpack(steps_ref, powers_ref)


def expand(packed):
    return pl.pallas_call(
        expand_kernel,
        out_shape=jax.ShapeDtypeStruct(packed[0].shape, f32),
        in_specs=[VMEM] * 2,
        out_specs=VMEM,
        compiler_params=PARAMS,
    )(*packed)


def project_kernel(*refs, step):
    steps_ref, powers_ref, gain_ref, weight_ref, out_ref, state_ref = refs
    state = unpack(steps_ref, powers_ref)
    state_ref[...] = state
    which = layer_of(step)
    scaled = (state * gain_ref[pl.ds(which, 1), :]).astype(bf16)
    raw = jnp.dot(scaled, weight_ref[0, which], preferred_element_type=f32)
    write_pieces(out_ref, raw, state)


def project(packed, gain, weight, step):
    rows, width = packed[0].shape
    return pl.pallas_call(
        functools.partial(project_kernel, step=step),
        out_shape=(
            jax.ShapeDtypeStruct((2 * rows // TREE, TREE, PIECE), bf16),
            jax.ShapeDtypeStruct((rows, width), f32),
        ),
        in_specs=[VMEM] * (2 + len(packed)),
        out_specs=(VMEM,) * 2,
        compiler_params=PARAMS,
    )(*packed, gain, weight)


def attend_kernel(got_ref, table_ref, cache_ref, *refs, step):
    *sides_ref, out_ref = refs
    total = jnp.sum(got_ref[:, :, :PIECE].astype(f32), axis=0)
    square = total[:, MIX : MIX + 1] + total[:, MIX + HEAD // 2 : MIX + HEAD // 2 + 1]
    factor = lax.rsqrt(square / D + epsilon)
    projected = (total[:, :MIX] * factor).astype(bf16)
    heads = HALF // HEAD
    queries = jnp.concatenate(
        [projected[:, h * HEAD : (h + 1) * HEAD] for h in range(heads)], axis=0
    )
    tree_keys = projected[:, HALF : HALF + HEAD]
    tree_values = projected[:, HALF + HEAD :]
    if step:
        mine_ref, come_ref = sides_ref
        blocks = [
            [
                side_ref[piece, :, start : start + HEAD]
                for piece in range(side_ref.shape[0])
                for start in range(0, side_ref.shape[2], HEAD)
            ]
            for side_ref in (mine_ref, come_ref)
        ]
    else:
        blocks = [
            [
                got_ref[piece, :, start + side * HEAD : start + (side + 1) * HEAD]
                for piece in range(got_ref.shape[0])
                for start in range(PIECE, got_ref.shape[2], BOTH)
            ]
            for side in range(2)
        ]
    keys, values = (jnp.concatenate(block, axis=0) for block in blocks)
    if step:
        swapped = lax.rem(lax.axis_index("tensor"), 2) == 1
        keys, values = jnp.where(swapped, values, keys), jnp.where(swapped, keys, values)
    contract = (((1,), (1,)), ((), ()))
    scaling = HEAD ** (-0.5)
    scores = lax.dot_general(queries, keys, contract, preferred_element_type=f32)
    tree_scores = lax.dot_general(queries, tree_keys, contract, preferred_element_type=f32)
    position = lax.broadcasted_iota(jnp.int32, scores.shape, 1)
    table = table_ref[step]
    live = table[0:1, TREE : TREE + 1].astype(jnp.int32)
    visible = jnp.concatenate([table[:, :TREE]] * heads, axis=0) > 0.5
    scores = jnp.where(position < live, scores * scaling, lowest)
    tree_scores = jnp.where(visible, tree_scores * scaling, lowest)
    row_max = jnp.maximum(
        jnp.max(scores, axis=-1, keepdims=True), jnp.max(tree_scores, axis=-1, keepdims=True)
    )
    weights = jnp.exp(scores - row_max)
    tree_weights = jnp.exp(tree_scores - row_max)
    row_sum = jnp.sum(weights, axis=-1, keepdims=True) + jnp.sum(
        tree_weights, axis=-1, keepdims=True
    )
    weighted = jnp.dot(weights.astype(bf16), values, preferred_element_type=f32)
    weighted = weighted + jnp.dot(
        tree_weights.astype(bf16), tree_values, preferred_element_type=f32
    )
    attended = (weighted / row_sum).astype(bf16)
    for h in range(heads):
        part = attended[h * TREE : (h + 1) * TREE]
        for piece in range(out_ref.shape[0]):
            out_ref[piece, :, h * HEAD : (h + 1) * HEAD] = part
    if step + 1 < cache_ref.shape[0]:
        write_sides(out_ref, cache_ref, step + 1, HALF)


def attend(got, table, cache, step, sides=()):
    steps, _, span = cache.shape[:3]
    width = HALF + (span // TREE * HEAD if step + 1 < steps else 0)
    return pl.pallas_call(
        functools.partial(attend_kernel, step=step),
        out_shape=jax.ShapeDtypeStruct((got.shape[0], TREE, width), bf16),
        in_specs=[VMEM] * (3 + len(sides)),
        out_specs=VMEM,
        compiler_params=PARAMS,
    )(got, table, cache, *sides)


def update_kernel(state_ref, got_ref, weight_ref, *refs, step, last):
    if last:
        out_refs = refs
    else:
        *out_refs, side_ref = refs
        side_ref[...] = got_ref[:, :, HALF:]
    attended = jnp.concatenate(
        [
            jnp.concatenate([got_ref[at, :, :HALF], got_ref[at + 1, :, :HALF]], axis=1)
            for at in range(0, got_ref.shape[0], 2)
        ],
        axis=0,
    )

    delta = jnp.dot(attended, weight_ref[0, layer_of(step)], preferred_element_type=f32)
    pack(*out_refs, state_ref[...] + delta)


def update(state, got, weight, step):
    rows, width = state.shape
    count, tree, total = got.shape
    out_shape = (
        jax.ShapeDtypeStruct((rows - TREE, width), jnp.int16),
        jax.ShapeDtypeStruct((TREE, width + HEAD), jnp.int16),
    )
    last = total == HALF
    if not last:
        out_shape += (jax.ShapeDtypeStruct((count, tree, total - HALF), bf16),)
    return pl.pallas_call(
        functools.partial(update_kernel, step=step, last=last),
        out_shape=out_shape,
        in_specs=[VMEM] * 3,
        out_specs=(VMEM,) * len(out_shape),
        compiler_params=PARAMS,
    )(state, got, weight)


def exchange(value):
    return lax.all_to_all(value, "tensor", 0, 0, tiled=True)


def far(value):
    return pltpu.with_memory_space_constraint(value, pltpu.HBM)


def body(hidden_in, norm_gain, w_qkv, w_out, kv_cache, parents, lengths, assign):
    sections = lax.axis_size("section")
    ring = [(s, (s + 1) % sections) for s in range(sections)]
    cache = kv_cache.reshape(kv_cache.shape[1:])
    pieces, state, table, gain = first(
        assign, parents, lengths, hidden_in, norm_gain, w_qkv, kv_cache
    )
    mates = [(t, t ^ 1) for t in range(pieces.shape[0])]
    for step in range(kv_cache.shape[1]):
        if step:
            pieces, state = project(packed, gain, w_qkv, step)
            pieces, come = lax.optimization_barrier((pieces, come))
            spread = attend(exchange(pieces), table, cache, step, (mine, come))
        else:
            spread = attend(exchange(pieces), table, cache, step)
        outs = update(state, exchange(spread), w_out, step)
        early, late = (lax.ppermute(part, "section", ring) for part in outs[:2])
        width = early.shape[1]
        packed = (jnp.concatenate([early, late[:, :width]]), late[:, width:])
        if len(outs) > 2:
            mine = outs[2]
            come = lax.ppermute(mine, "tensor", mates)
    return expand(packed).reshape(hidden_in.shape)


def solution(mesh):
    in_specs = (
        P(("dp", "section"), None, None, "tensor"),
        P(("dp", "section"), None, "tensor"),
        P(("dp", "section"), None, "tensor", None),
        P(("dp", "section"), None, None, "tensor"),
        P(("dp", "section"), None, None, "tensor", None),
        P("dp", None),
        P("dp"),
        P("dp", None),
    )
    out_specs = P(("dp", "section"), None, None, "tensor")
    return jax.shard_map(body, mesh=mesh, in_specs=in_specs, out_specs=out_specs, check_vma=False)
```
